512 devices in a mesh: grp: 16 (over y, z_lo), blk: 32 (over z_hi, x, core).
Axes of the slice: x: 4, y: 8, z: 8 (z_hi: 4, z_lo: 2; z = z_hi * 2 + z_lo), core: 2. Of those that a mesh axis runs over, the one named last changes fastest.
Arguments:
- image: bfloat16 [32, 2048, 1024], P('blk', 'grp')
- text: bfloat16 [32, 2048, 1024], P('blk', 'grp')
- logit_scale: float32 [], replicated, may hold values from 1.5 to 2.5
- lse_row: bfloat16 [32, 2048], P('blk', 'grp')
- lse_col: bfloat16 [32, 2048], P('blk', 'grp')
- pair: int32 [32, 2048], P('blk', 'grp'), may hold values from 0 to 2047, each once within a row
Outputs:
- grad_image: bfloat16 [32, 2048, 1024], P('blk', 'grp')
- grad_text: bfloat16 [32, 2048, 1024], P('blk', 'grp')
The draws below stay inside these ranges and needn't reach their ends.
Inputs may be any that keep to these rules, and one draw needn't show every extreme that they name: Each row pair[b] is a permutation of 0 .. 2047.
All inputs are finite; a program needn't handle non-finite values.
Results may differ from the reference program's by a relative error of at most 0.022.
Values may be sent and summed in bfloat16 or wider, within the bound.
A program may use at most 64 MiB of HBM per device.

```python
import math
import jax
import jax.numpy as jnp
from jax import lax

E = 1024
ROWS_DEV = 128
STEPS = 2
BLOCKS = 32
ROWS_BLK = 2048
N_GRP = 16


def embed_values(key):
    values = jnp.clip(jax.random.normal(key, (BLOCKS, ROWS_BLK, E), jnp.float32), -4.0, 4.0)
    return (values * E ** (-0.25)).astype(jnp.bfloat16)


def lse_values(key):
    centre = 2.0 + math.log(STEPS * ROWS_BLK)
    values = jax.random.uniform(key, (BLOCKS, ROWS_BLK), jnp.float32, centre - 1.0, centre + 1.0)
    return values.astype(jnp.bfloat16)


def draw_image(key, part):
    key = jax.random.fold_in(key, 11)
    return embed_values(key)


def draw_text(key, part):
    key = jax.random.fold_in(key, 12)
    return embed_values(key)


def draw_lse_row(key, part):
    key = jax.random.fold_in(key, 13)
    return lse_values(key)


def draw_lse_col(key, part):
    key = jax.random.fold_in(key, 14)
    return lse_values(key)


def setup_inputs(seed: int = 0) -> dict:
    seeds = jax.random.split(jax.random.key(seed), 7)
    image = draw_image(jax.random.fold_in(seeds[6], 71), 0)
    text = draw_text(jax.random.fold_in(seeds[6], 71), 0)
    logit_scale = jnp.clip(jnp.exp(jax.random.uniform(seeds[2], (), jnp.float32, math.log(1.5), math.log(2.5))), 1.5, 2.5)
    lse_row = draw_lse_row(jax.random.fold_in(seeds[6], 71), 0)
    lse_col = draw_lse_col(jax.random.fold_in(seeds[6], 71), 0)
    pair = jax.vmap(lambda own: jax.random.permutation(own, ROWS_BLK))(jax.random.split(seeds[5], BLOCKS)).reshape((BLOCKS, ROWS_BLK)).astype(jnp.int32)
    return dict(image=image, text=text, logit_scale=logit_scale, lse_row=lse_row, lse_col=lse_col, pair=pair)


def score_grad(img, lrow, txt, lcol, pairs, scale, own):
    scores = lax.dot_general(img, txt, (((1,), (1,)), ((), ())), preferred_element_type=jnp.float32) * scale
    row_lse = lrow.astype(jnp.float32)
    col_lse = lcol.astype(jnp.float32)
    dscore = 0.5 * (jnp.exp(scores - row_lse[:, None]) + jnp.exp(scores - col_lse[None, :]))
    if own:
        columns = jnp.arange(txt.shape[0], dtype=jnp.int32)
        dscore = dscore - (pairs[:, None] == columns[None, :]).astype(jnp.float32)
    return dscore.astype(jnp.bfloat16)

def reference(image, text, logit_scale, lse_row, lse_col, pair):
    blocks = image.shape[0]
    width = image.shape[2]
    rows_blk = image.shape[1]

    def image_block(b):
        img = lax.dynamic_index_in_dim(image, b, 0, keepdims=False)
        lrow = lax.dynamic_index_in_dim(lse_row, b, 0, keepdims=False)
        pairs = lax.dynamic_index_in_dim(pair, b, 0, keepdims=False)
        total = jnp.zeros((rows_blk, width), jnp.float32)
        for k in range(STEPS):
            c = ((b + k) % blocks).astype(jnp.int32)
            txt = lax.dynamic_index_in_dim(text, c, 0, keepdims=False)
            lcol = lax.dynamic_index_in_dim(lse_col, c, 0, keepdims=False)
            dscore = score_grad(img, lrow, txt, lcol, pairs, logit_scale, k == 0)
            total = total + logit_scale * jnp.dot(dscore, txt, preferred_element_type=jnp.float32)
        return total.astype(jnp.bfloat16)

    def text_block(c):
        txt = lax.dynamic_index_in_dim(text, c, 0, keepdims=False)
        lcol = lax.dynamic_index_in_dim(lse_col, c, 0, keepdims=False)
        total = jnp.zeros((N_GRP, rows_blk, width), jnp.float32)
        for k in range(STEPS):
            b = ((c - k + blocks) % blocks).astype(jnp.int32)
            img = lax.dynamic_index_in_dim(image, b, 0, keepdims=False)
            lrow = lax.dynamic_index_in_dim(lse_row, b, 0, keepdims=False)
            pairs = lax.dynamic_index_in_dim(pair, b, 0, keepdims=False)
            dscore = score_grad(img, lrow, txt, lcol, pairs, logit_scale, k == 0)
            split_grad = dscore.reshape(N_GRP, ROWS_DEV, rows_blk).astype(jnp.float32)
            split_img = img.reshape(N_GRP, ROWS_DEV, width).astype(jnp.float32)
            total = total + logit_scale * jnp.einsum('grj,gre->gje', split_grad, split_img)
        shares = lax.optimization_barrier(total.astype(jnp.bfloat16)).astype(jnp.float32)
        return lax.optimization_barrier(jnp.sum(shares, axis=0)).astype(jnp.bfloat16)
    indices = jnp.arange(blocks, dtype=jnp.int32)
    grad_image = lax.map(image_block, indices)
    grad_text = lax.map(text_block, indices)
    return (grad_image, grad_text)
```

```python
import functools

import jax
import jax.numpy as jnp
from jax import lax
from jax.experimental import pallas as pl
from jax.experimental.pallas import tpu as pltpu
from jax.sharding import PartitionSpec as P

MESH = pl.DeviceIdType.MESH
RING = 8
ROWS = 128
PARTS = 4
CHUNK = ROWS // PARTS
HALF = PARTS // 2
PLACES = 8
NEAR = ((0, 1), (2, 3))
F32 = jnp.float32
BF16 = jnp.bfloat16


def place(direction, hops):
    return 0 if hops == 0 else 7 if hops == 4 else 2 * hops - 1 + direction


def gather_order(direction):
    first, second = NEAR[direction], NEAR[1 - direction]
    order = [(hop, part) for hop in (1, 2, 3) for part in first + second]
    return order + [(4, part) for part in first]


def reduce_order(direction):
    far, near = NEAR[direction], NEAR[1 - direction]
    order = [(3, near), (4, far), (2, near), (3, far), (1, near), (2, far), (1, far)]
    return [(hops, part) for hops, parts in order for part in parts]


def kernel(
    image, text, scale_ref, lrow_ref, lcol_ref, pair_ref, gi_out, gt_out,
    txt, img, meta, col, lct, dt, ct, rsend, rrecv, g0, gis, gir, zs, zr, oi, ot,
    local_sem, out_sem, ag_s, ag_r, rs_s, rs_r, im_s, im_r, me_s, me_r, co_s, co_r, gi_s, gi_r, zz_s, zz_r,
):
    g = lax.axis_index("grp")
    b = lax.axis_index("blk")
    n_blk = lax.axis_size("blk")
    n_grp = 2 * RING
    zpart = g + 1 - 2 * lax.rem(g, 2)
    nxt = lax.rem(b + 1, n_blk)
    prv = lax.rem(b + n_blk - 1, n_blk)
    ring = [lax.rem(g + 2 * i, n_grp) for i in range(RING)]
    side = [ring[1], ring[7]]
    scale = scale_ref[0]

    def send(src, dst, s_sem, r_sem, **to):
        copy = pltpu.make_async_remote_copy(
            src_ref=src, dst_ref=dst, send_sem=s_sem, recv_sem=r_sem,
            device_id={"grp": to.get("grp", g), "blk": to.get("blk", b)}, device_id_type=MESH,
        )
        return copy

    own_txt = pltpu.make_async_copy(text.at[0], txt.at[pl.ds(0, ROWS)], local_sem.at[0])
    own_img = pltpu.make_async_copy(image.at[0], img.at[pl.ds(0, ROWS)], local_sem.at[1])
    own_txt.start()
    own_img.start()

    barrier = pltpu.get_barrier_semaphore()
    for i in range(1, RING):
        pl.semaphore_signal(barrier, inc=1, device_id={"grp": ring[i], "blk": b}, device_id_type=MESH)
    pl.semaphore_signal(barrier, inc=1, device_id={"grp": zpart, "blk": b}, device_id_type=MESH)
    pl.semaphore_signal(barrier, inc=1, device_id={"grp": g, "blk": nxt}, device_id_type=MESH)
    pl.semaphore_signal(barrier, inc=1, device_id={"grp": g, "blk": prv}, device_id_type=MESH)

    meta[0] = jnp.zeros((8, ROWS), F32)
    meta[0, 0:1, :] = lrow_ref[...].astype(F32)
    meta[0, 1:2, :] = pair_ref[...].astype(F32)
    col[0] = jnp.broadcast_to(lcol_ref[...].astype(F32), (8, ROWS))
    own_txt.wait()
    own_img.wait()
    pl.semaphore_wait(barrier, RING - 1 + 3)

    started = []

    def go(copy):
        copy.start()
        started.append(copy)
        return copy

    orders = [gather_order(0), gather_order(1)]

    def gather_copy(direction, n):
        hop, part = orders[direction][n]
        rows = lambda p: txt.at[pl.ds(p * ROWS + part * CHUNK, CHUNK)]
        return send(
            rows(place(direction, hop - 1)), rows(place(direction, hop)),
            ag_s.at[direction, n], ag_r.at[direction, n], grp=side[direction],
        )

    gather = [[gather_copy(d, n) for n in range(len(orders[d]))] for d in range(2)]
    for n in range(PARTS):
        for d in range(2):
            go(gather[d][n])

    half = ROWS // 2
    z_img = go(send(img.at[pl.ds(0, ROWS)], img.at[pl.ds(ROWS, ROWS)], im_s.at[0], im_r.at[0], grp=zpart))
    z_meta = go(send(meta.at[0], meta.at[1], me_s.at[0], me_r.at[0], grp=zpart))
    x_img = go(send(img.at[pl.ds(0, ROWS)], img.at[pl.ds(2 * ROWS, ROWS)], im_s.at[1], im_r.at[1], blk=nxt))
    x_meta = go(send(meta.at[0], meta.at[2], me_s.at[1], me_r.at[1], blk=nxt))
    cols = []
    for i in range(1, RING):
        there = 7 if i == 4 else 2 * i - 1 if i < 4 else 2 * (RING - i)
        cols.append(go(send(col.at[0], col.at[there], co_s.at[i - 1], co_r.at[there - 1], grp=ring[i])))

    def arrived(n):
        for d in range(2):
            gather[d][n].wait_recv()
            if n + PARTS < len(orders[d]):
                go(gather[d][n + PARTS])

    def scores(p0, count, k):
        t = txt[p0 * ROWS : (p0 + count) * ROWS, :]
        s = lax.dot_general(
            t, img[k * 2 * ROWS : (k + 1) * 2 * ROWS, :], (((1,), (1,)), ((), ())), preferred_element_type=F32
        )
        lr = jnp.concatenate([meta[2 * k, 0:1, :], meta[2 * k + 1, 0:1, :]], axis=1)
        for i in range(count):
            p = p0 + i
            si = s[i * ROWS : (i + 1) * ROWS] * scale
            if k == 0:
                lct[p * ROWS : (p + 1) * ROWS, :] = jnp.broadcast_to(col[p, 0:1, :], (ROWS, ROWS)).T
            lc = lct[p * ROWS : (p + 1) * ROWS, :]
            lc = jnp.concatenate([lc, lc], axis=1)
            d = 0.5 * (jnp.exp(si - lr) + jnp.exp(si - lc))
            if k == 0:
                rel = 0 if p == 0 else 4 if p == 7 else (RING - (p + 1) // 2) if p % 2 else p // 2
                pr = jnp.concatenate([meta[0, 1:2, :], meta[1, 1:2, :]], axis=1).astype(jnp.int32)
                row = ring[rel] * ROWS + lax.broadcasted_iota(jnp.int32, (ROWS, 2 * ROWS), 0)
                d = d - (pr == row).astype(F32)
            dt[p * ROWS : (p + 1) * ROWS, k * 2 * ROWS : (k + 1) * 2 * ROWS] = d.astype(BF16)

    def contribution(p0, count):
        rows = slice(p0 * ROWS, (p0 + count) * ROWS)
        ct[rows, :] = jnp.dot(dt[rows, :], img[...], preferred_element_type=F32)

    def image_term(k):
        return lax.dot_general(
            dt[:, k * 2 * ROWS : (k + 1) * 2 * ROWS], txt[...], (((0,), (0,)), ((), ())), preferred_element_type=F32
        )

    r_orders = [reduce_order(0), reduce_order(1)]

    def reduce_copy(direction, n):
        rows = pl.ds(n * CHUNK, CHUNK)
        return send(
            rsend.at[direction, rows], rrecv.at[direction, rows],
            rs_s.at[direction, n], rs_r.at[direction, n], grp=side[direction],
        )

    reduction = [[reduce_copy(d, n) for n in range(len(r_orders[d]))] for d in range(2)]

    def reduce_step(n):
        for d in range(2):
            hops, part = r_orders[d][n]
            start = place(1 - d, hops) * ROWS + part * CHUNK
            total = ct[start : start + CHUNK, :]
            if (hops + 1, part) in r_orders[d]:
                m = r_orders[d].index((hops + 1, part))
                reduction[d][m].wait_recv()
                total = total + rrecv[d, m * CHUNK : (m + 1) * CHUNK, :].astype(F32)
            rsend[d, n * CHUNK : (n + 1) * CHUNK, :] = total.astype(BF16)
            go(reduction[d][n])

    for n in range(4):
        arrived(n)
    z_img.wait_recv()
    z_meta.wait_recv()
    x_img2 = go(send(img.at[pl.ds(ROWS, ROWS)], img.at[pl.ds(3 * ROWS, ROWS)], im_s.at[2], im_r.at[2], blk=nxt))
    x_meta2 = go(send(meta.at[1], meta.at[3], me_s.at[2], me_r.at[2], blk=nxt))
    for copy in cols:
        copy.wait_recv()
    scores(0, 1, 0)
    arrived(4)
    scores(1, 2, 0)
    for n in (5, 6, 7):
        arrived(n)
    scores(3, 2, 0)
    arrived(8)
    arrived(9)
    for copy in (x_img, x_meta, x_img2, x_meta2):
        copy.wait_recv()
    scores(0, 1, 1)
    scores(1, 2, 1)
    arrived(10)
    scores(3, 2, 1)
    contribution(0, 1)
    arrived(11)
    scores(5, 2, 0)
    scores(5, 2, 1)
    contribution(5, 2)
    reduce_step(0)
    reduce_step(1)
    arrived(12)
    arrived(13)
    scores(7, 1, 0)
    scores(7, 1, 1)
    contribution(7, 1)
    reduce_step(2)
    reduce_step(3)

    gis[...] = image_term(1).astype(BF16)
    back = [
        go(send(gis.at[rows], gir.at[rows], gi_s.at[i], gi_r.at[i], blk=prv))
        for i, rows in enumerate((pl.ds(ROWS, ROWS), pl.ds(0, ROWS)))
    ]
    contribution(3, 2)
    reduce_step(4)
    reduce_step(5)
    contribution(1, 2)
    g0[...] = image_term(0)
    for n in (6, 7, 8, 9):
        reduce_step(n)
    back[0].wait_recv()
    zs[...] = (g0[ROWS:, :] + gir[ROWS:, :].astype(F32)).astype(BF16)
    z_grad = go(send(zs, zr, zz_s, zz_r, grp=zpart))
    back[1].wait_recv()
    for n in (10, 11):
        reduce_step(n)
    z_grad.wait_recv()
    oi[...] = (scale * (g0[:ROWS, :] + gir[:ROWS, :].astype(F32) + zr[...].astype(F32))).astype(BF16)
    out_i = pltpu.make_async_copy(oi, gi_out.at[0], out_sem.at[0])
    out_i.start()
    for n in (12, 13):
        reduce_step(n)
    for part in NEAR[1] + NEAR[0]:
        total = ct[part * CHUNK : (part + 1) * CHUNK, :]
        for d in range(2):
            m = r_orders[d].index((1, part))
            reduction[d][m].wait_recv()
            total = total + rrecv[d, m * CHUNK : (m + 1) * CHUNK, :].astype(F32)
        ot[part * CHUNK : (part + 1) * CHUNK, :] = (scale * total).astype(BF16)
    out_t = pltpu.make_async_copy(ot, gt_out.at[0], out_sem.at[1])
    out_t.start()
    for copy in started:
        copy.wait_send()
    out_i.wait()
    out_t.wait()


def body(image, text, logit_scale, lse_row, lse_col, pair):
    width = image.shape[2]
    msgs = 3 * PARTS + HALF
    any_spec = pl.BlockSpec(memory_space=pl.ANY)
    vmem = pl.BlockSpec(memory_space=pltpu.VMEM)
    dma = pltpu.SemaphoreType.DMA
    out = jax.ShapeDtypeStruct((1, ROWS, width), BF16)
    return pl.pallas_call(
        kernel,
        out_shape=(out, out),
        in_specs=[any_spec, any_spec, pl.BlockSpec(memory_space=pltpu.SMEM), vmem, vmem, vmem],
        out_specs=(any_spec, any_spec),
        scratch_shapes=[
            pltpu.VMEM((PLACES * ROWS, width), BF16),
            pltpu.VMEM((4 * ROWS, width), BF16),
            pltpu.VMEM((4, 8, ROWS), F32),
            pltpu.VMEM((PLACES, 8, ROWS), F32),
            pltpu.VMEM((PLACES * ROWS, ROWS), F32),
            pltpu.VMEM((PLACES * ROWS, 4 * ROWS), BF16),
            pltpu.VMEM((PLACES * ROWS, width), F32),
            pltpu.VMEM((2, msgs * CHUNK, width), BF16),
            pltpu.VMEM((2, msgs * CHUNK, width), BF16),
            pltpu.VMEM((2 * ROWS, width), F32),
            pltpu.VMEM((2 * ROWS, width), BF16),
            pltpu.VMEM((2 * ROWS, width), BF16),
            pltpu.VMEM((ROWS, width), BF16),
            pltpu.VMEM((ROWS, width), BF16),
            pltpu.VMEM((ROWS, width), BF16),
            pltpu.VMEM((ROWS, width), BF16),
            dma((2,)),
            dma((2,)),
            dma((2, msgs)),
            dma((2, msgs)),
            dma((2, msgs)),
            dma((2, msgs)),
            dma((3,)),
            dma((3,)),
            dma((3,)),
            dma((3,)),
            dma((RING - 1,)),
            dma((RING - 1,)),
            dma((2,)),
            dma((2,)),
            dma,
            dma,
        ],
        compiler_params=pltpu.CompilerParams(
            collective_id=0, has_side_effects=True, vmem_limit_bytes=48 * 2**20
        ),
        cost_estimate=pl.CostEstimate(
            flops=12 * ROWS * 16 * ROWS * width, bytes_accessed=8 * ROWS * width, transcendentals=8 * ROWS * 16 * ROWS
        ),
    )(image, text, jnp.reshape(logit_scale, (1,)), lse_row, lse_col, pair)


def solution(mesh):
    return jax.shard_map(
        body,
        mesh=mesh,
        in_specs=(
            P("blk", "grp", None),
            P("blk", "grp", None),
            P(),
            P("blk", "grp"),
            P("blk", "grp"),
            P("blk", "grp"),
        ),
        out_specs=(P("blk", "grp", None), P("blk", "grp", None)),
        check_vma=False,
    )
```

```python
import functools

import jax
import jax.numpy as jnp
from jax import lax
from jax.experimental import pallas as pl
from jax.experimental.pallas import tpu as pltpu
from jax.sharding import PartitionSpec as P

MESH = pl.DeviceIdType.MESH
RING = 8
ROWS = 128
PARTS = 4
CHUNK = ROWS // PARTS
HALF = ROWS // 2
PLACES = 8
RUN = 8
FAR = ((2, 3), (1, 0))
F32 = jnp.float32
BF16 = jnp.bfloat16


def place(direction, hops):
    return 0 if hops == 0 else 7 if hops == 4 else 2 * hops - 1 + direction


def gather_order(direction):
    far, near = FAR[direction], FAR[1 - direction]
    order = [(hop, part) for hop in (1, 2, 3) for part in far + near]
    return order + [(4, part) for part in far]


def reduce_order(direction):
    f0, f1 = FAR[direction]
    n0, n1 = FAR[1 - direction]
    return [
        (3, n0), (3, n1), (4, f0), (4, f1), (2, n0), (3, f0), (3, f1),
        (2, n1), (2, f0), (2, f1), (1, n0), (1, f0), (1, f1), (1, n1),
    ]


def kernel(
    image, text, scale_ref, lrow_ref, lcol_ref, pair_ref, gi_out, gt_out,
    txt, img, meta, col, lct, dt, ct, rsend, rrecv, g0, g1, gis, gir, zs, zr, vecs, pairs, oi, ot,
    local_sem, out_sem, ag_s, ag_r, rs_s, rs_r, im_s, im_r, me_s, me_r, co_s, co_r, gi_s, gi_r, zz_s, zz_r,
):
    g = lax.axis_index("grp")
    b = lax.axis_index("blk")
    n_blk = lax.axis_size("blk")
    n_grp = 2 * RING
    zpart = g + 1 - 2 * lax.rem(g, 2)
    nxt = lax.rem(b + 1, n_blk)
    prv = lax.rem(b + n_blk - 1, n_blk)
    ring = [lax.rem(g + 2 * i, n_grp) for i in range(RING)]
    side = [ring[1], ring[7]]
    z_lo = lax.rem(g, 2)
    last = lax.rem(b, RUN) == RUN - 1
    first = lax.rem(b, RUN) == 0
    zero = b == 0
    has_next = jnp.logical_not(jnp.logical_and(last, z_lo == 0))
    has_prev = jnp.logical_not(jnp.logical_and(first, z_lo == 1))
    outlet = jnp.logical_and(last, z_lo == 1)
    inlet = jnp.logical_and(first, z_lo == 0)
    next_grp = jnp.where(last, zpart, g)
    prev_grp = jnp.where(first, zpart, g)

    barrier = pltpu.get_barrier_semaphore()

    def greet(grp, blk):
        pl.semaphore_signal(barrier, inc=1, device_id={"grp": grp, "blk": blk}, device_id_type=MESH)

    greet(side[0], b)
    greet(side[1], b)
    greet(zpart, b)

    @pl.when(has_prev)
    def _():
        greet(prev_grp, prv)

    def copy_to(src, dst, s_sem, r_sem, grp=g, blk=b):
        return pltpu.make_async_remote_copy(
            src_ref=src, dst_ref=dst, send_sem=s_sem, recv_sem=r_sem,
            device_id={"grp": grp, "blk": blk}, device_id_type=MESH,
        )

    local = [
        pltpu.make_async_copy(src, dst, local_sem.at[i])
        for i, (src, dst) in enumerate((
            (pair_ref, pairs),
            (lrow_ref, vecs.at[0]),
            (lcol_ref, vecs.at[1]),
            (text.at[0], txt.at[pl.ds(0, ROWS)]),
            (image.at[0], img.at[pl.ds(0, ROWS)]),
        ))
    ]
    for copy in local:
        copy.start()
    scale = scale_ref[0]
    started = []

    def go(copy):
        copy.start()
        started.append(copy)
        return copy

    orders = [gather_order(0), gather_order(1)]

    def gather_copy(direction, n):
        hop, part = orders[direction][n]
        rows = lambda p: txt.at[pl.ds(p * ROWS + part * CHUNK, CHUNK)]
        src = text.at[0, pl.ds(part * CHUNK, CHUNK)] if hop == 1 else rows(place(direction, hop - 1))
        return copy_to(
            src, rows(place(direction, hop)), ag_s.at[direction, n], ag_r.at[direction, n], grp=side[direction]
        )

    def col_copy(direction, hop):
        return copy_to(
            col.at[place(direction, hop - 1)], col.at[place(direction, hop)],
            co_s.at[direction, hop - 1], co_r.at[direction, hop - 1], grp=side[direction],
        )

    gather = [[gather_copy(d, n) for n in range(len(orders[d]))] for d in range(2)]
    cols = [[col_copy(0, hop) for hop in (1, 2, 3, 4)], [col_copy(1, hop) for hop in (1, 2, 3)]]

    def arrived(*steps):
        for n in steps:
            hop = n // PARTS + 1
            for d in range(2):
                gather[d][n].wait_recv()
                if n + PARTS < len(orders[d]):
                    go(gather[d][n + PARTS])
            for d in range(2):
                if n % PARTS == (2 if hop < 4 else 0) and hop <= len(cols[d]):
                    cols[d][hop - 1].wait_recv()
                    if hop < len(cols[d]):
                        go(cols[d][hop])

    def image_copies(src, dst, sem, **to):
        def copy(i):
            start = i * HALF
            rows = image.at[0, pl.ds(start, HALF)] if src == 0 else img.at[pl.ds(src * ROWS + start, HALF)]
            r_sem = im_r.at[2 * (dst - 1) + i]
            return copy_to(rows, img.at[pl.ds(dst * ROWS + start, HALF)], im_s.at[2 * sem + i], r_sem, **to)

        return copy(0), copy(1), copy_to(meta.at[src], meta.at[dst], me_s.at[sem], me_r.at[dst - 1], **to)

    swap = last.astype(jnp.int32)
    z_img = image_copies(0, 1, 0, grp=zpart)
    next_own = image_copies(0, 2 + swap, 1, grp=next_grp, blk=nxt)
    next_other = image_copies(1, 3 - swap, 2, grp=next_grp, blk=nxt)
    passed = {3: image_copies(3, 2, 3, grp=zpart), 2: image_copies(2, 3, 4, grp=zpart)}
    arrivals = {2: image_copies(0, 2, 0, grp=zpart), 3: image_copies(0, 3, 0, grp=zpart)}

    def image_arrived(slot):
        for copy in arrivals[slot]:
            copy.wait_recv()

    def start_if(condition, copies):
        @pl.when(condition)
        def _():
            for copy in copies:
                copy.start()

    def pass_on(condition, slot):
        @pl.when(condition)
        def _():
            for got, copy in zip(arrivals[slot], passed[slot]):
                got.wait_recv()
                copy.start()

    def take(ref, parts):
        pieces = []
        for p, part in parts:
            lo = p * ROWS + part * CHUNK
            if pieces and pieces[-1][1] == lo:
                pieces[-1][1] = lo + CHUNK
            else:
                pieces.append([lo, lo + CHUNK])
        pieces = [ref[lo:hi, :] for lo, hi in pieces]
        return pieces[0] if len(pieces) == 1 else jnp.concatenate(pieces, axis=0)

    def whole(*places):
        return [(p, part) for p in places for part in range(PARTS)]

    def columns(*places):
        for p in places:
            lct[p * ROWS : (p + 1) * ROWS, :] = jnp.broadcast_to(col[p, 0:1, :], (ROWS, ROWS)).T

    def scores(parts, k):
        s = lax.dot_general(
            take(txt, parts), img[k * 2 * ROWS : (k + 1) * 2 * ROWS, :], (((1,), (1,)), ((), ())),
            preferred_element_type=F32,
        )
        s = s * scale
        lr = jnp.concatenate([meta[2 * k, 0:1, :], meta[2 * k + 1, 0:1, :]], axis=1)
        lc = take(lct, parts)
        d = 0.5 * (jnp.exp(s - lr) + jnp.exp(s - jnp.concatenate([lc, lc], axis=1)))
        if k == 0:
            pr = jnp.concatenate([meta[0, 1:2, :], meta[1, 1:2, :]], axis=1).astype(jnp.int32)
            iota = lax.broadcasted_iota(jnp.int32, (CHUNK, 2 * ROWS), 0)
        for i, (p, part) in enumerate(parts):
            rows = d[i * CHUNK : (i + 1) * CHUNK]
            if k == 0:
                rel = 0 if p == 0 else 4 if p == 7 else (RING - (p + 1) // 2) if p % 2 else p // 2
                rows = rows - (pr - (ring[rel] * ROWS + part * CHUNK) == iota).astype(F32)
            lo = p * ROWS + part * CHUNK
            dt[lo : lo + CHUNK, k * 2 * ROWS : (k + 1) * 2 * ROWS] = rows.astype(BF16)

    def contribution(parts):
        c = jnp.dot(take(dt, parts), img[...], preferred_element_type=F32)
        for i, (p, part) in enumerate(parts):
            lo = p * ROWS + part * CHUNK
            ct[lo : lo + CHUNK, :] = c[i * CHUNK : (i + 1) * CHUNK]

    def image_term(k):
        return lax.dot_general(
            dt[:, k * 2 * ROWS : (k + 1) * 2 * ROWS], txt[...], (((0,), (0,)), ((), ())), preferred_element_type=F32
        )

    r_orders = [reduce_order(0), reduce_order(1)]

    def reduce_copy(direction, n):
        rows = pl.ds(n * CHUNK, CHUNK)
        return copy_to(
            rsend.at[direction, rows], rrecv.at[direction, rows],
            rs_s.at[direction, n], rs_r.at[direction, n], grp=side[direction],
        )

    reduction = [[reduce_copy(d, n) for n in range(len(r_orders[d]))] for d in range(2)]

    def reduce_step(*steps):
        for n in steps:
            for d in range(2):
                hops, part = r_orders[d][n]
                start = place(1 - d, hops) * ROWS + part * CHUNK
                total = ct[start : start + CHUNK, :]
                if (hops + 1, part) in r_orders[d]:
                    m = r_orders[d].index((hops + 1, part))
                    reduction[d][m].wait_recv()
                    total = total + rrecv[d, m * CHUNK : (m + 1) * CHUNK, :].astype(F32)
                rsend[d, n * CHUNK : (n + 1) * CHUNK, :] = total.astype(BF16)
                go(reduction[d][n])

    half = lambda j: slice(j * HALF, (j + 1) * HALF)
    feeder = jnp.logical_and(first, z_lo == 1)
    back_blk = jnp.where(feeder, b, prv)

    def back_copy(j):
        if j < 2:
            to = jnp.where(feeder, j + 6, jnp.where(inlet, j + 2, j))
        else:
            to = jnp.where(feeder, j + 2, jnp.where(inlet, j - 2, j))
        return copy_to(
            gis.at[pl.ds(j * HALF, HALF)], gir.at[pl.ds(pl.multiple_of(to * HALF, HALF), HALF)],
            gi_s.at[j], gi_r.at[to], grp=prev_grp, blk=back_blk,
        )

    back = [back_copy(j) for j in range(4)]

    def back_wait(to):
        rows = pl.ds(to * HALF, HALF)
        copy_to(gis.at[pl.ds(0, HALF)], gir.at[rows], gi_s.at[0], gi_r.at[to], grp=zpart).wait_recv()

    def inlet_back(j):
        @pl.when(inlet)
        def _():
            back_wait(4 + j)
            gis[half(j), :] = (g1[half(j), :] + gir[half(4 + j), :].astype(F32)).astype(BF16)
            back[j].start()

    z_own = [
        copy_to(zs.at[pl.ds(i * HALF, HALF)], zr.at[pl.ds(i * HALF, HALF)], zz_s.at[i], zz_r.at[i], grp=zpart)
        for i in range(2)
    ]

    def own_back(condition):
        @pl.when(condition)
        def _():
            for i in range(2):

                @pl.when(has_next)
                def _():
                    back_wait(2 + i)

                zs[half(i), :] = (g0[half(2 + i), :] + gir[half(2 + i), :].astype(F32)).astype(BF16)
                z_own[i].start()

    pl.semaphore_wait(barrier, 3 + has_next.astype(jnp.int32))
    for n in range(PARTS):
        for d in range(2):
            go(gather[d][n])
    start_if(True, z_img[:2])
    start_if(has_next, next_own[:2])
    for copy in local[:3]:
        copy.wait()
    meta[0] = jnp.zeros((8, ROWS), F32)
    meta[0, 0:1, :] = vecs[0].astype(F32)
    meta[0, 1:2, :] = pairs[...].astype(F32)
    col[0] = jnp.broadcast_to(vecs[1].astype(F32), (8, ROWS))
    start_if(True, z_img[2:])
    start_if(has_next, next_own[2:])
    for d in range(2):
        go(cols[d][0])
    for copy in local[3:]:
        copy.wait()
    columns(0)
    arrived(0, 1)

    @pl.when(outlet)
    def _():
        for got, copy in zip(z_img, next_other):
            got.wait_recv()
            copy.start()

    arrived(2)
    pass_on(jnp.logical_and(inlet, jnp.logical_not(zero)), 3)
    arrived(3)

    @pl.when(jnp.logical_not(outlet))
    def _():
        for copy in z_img:
            copy.wait_recv()

    start_if(jnp.logical_not(last), next_other)
    columns(1, 2)
    scores(whole(0), 0)
    arrived(4)
    pass_on(jnp.logical_and(inlet, jnp.logical_not(zero)), 2)
    scores(whole(1, 2), 0)
    arrived(5, 6, 7)
    pass_on(jnp.logical_and(inlet, zero), 3)
    columns(3, 4)
    scores(whole(3, 4), 0)
    arrived(8, 9)
    pass_on(jnp.logical_and(inlet, zero), 2)
    near = [(5, part) for part in FAR[0]] + [(6, part) for part in FAR[1]]
    far = [(5, part) for part in FAR[1]] + [(6, part) for part in FAR[0]]
    arrived(10)
    columns(5, 6)
    scores(near, 0)

    @pl.when(jnp.logical_not(inlet))
    def _():
        image_arrived(2)
        image_arrived(3)

    scores(near, 1)
    contribution(near)
    reduce_step(0, 1)
    scores(whole(0), 1)
    scores(whole(1, 2), 1)
    arrived(11)
    scores(whole(3, 4), 1)
    scores(far, 0)
    scores(far, 1)
    arrived(12)
    columns(7)
    opposite = sorted([(7, FAR[0][0]), (7, FAR[1][0])])
    scores(opposite, 0)
    scores(opposite, 1)
    contribution(opposite)
    reduce_step(2)
    arrived(13)
    opposite = sorted([(7, FAR[0][1]), (7, FAR[1][1])])
    scores(opposite, 0)
    scores(opposite, 1)
    contribution(opposite)
    reduce_step(3)
    g1[...] = image_term(1)

    @pl.when(jnp.logical_not(inlet))
    def _():
        for j in (2, 3, 0, 1):
            gis[half(j), :] = g1[half(j), :].astype(BF16)
            back[j].start()

    @pl.when(jnp.logical_not(has_next))
    def _():
        gir[0 : 2 * ROWS, :] = jnp.zeros((2 * ROWS, gir.shape[1]), BF16)

    contribution(whole(3, 4))
    reduce_step(4)
    contribution(far)
    reduce_step(5, 6)
    contribution(whole(1, 2))
    g0[...] = image_term(0)
    contribution(whole(0))
    reduce_step(7, 8)
    own_back(jnp.logical_not(last))
    inlet_back(0)
    reduce_step(9)
    inlet_back(1)
    reduce_step(10)
    inlet_back(2)
    reduce_step(11)
    inlet_back(3)
    reduce_step(12, 13)
    own_back(last)

    @pl.when(has_next)
    def _():
        back_wait(0)
        back_wait(1)

    for copy in z_own:
        copy.wait_recv()
    oi[...] = (scale * (g0[:ROWS, :] + gir[:ROWS, :].astype(F32) + zr[...].astype(F32))).astype(BF16)
    outs = [pltpu.make_async_copy(oi, gi_out.at[0], out_sem.at[0])]
    outs[0].start()
    for part in sorted(range(PARTS), key=lambda part: r_orders[0].index((1, part)) + r_orders[1].index((1, part))):
        rows = pl.ds(part * CHUNK, CHUNK)
        total = ct[part * CHUNK : (part + 1) * CHUNK, :]
        for d in range(2):
            m = r_orders[d].index((1, part))
            reduction[d][m].wait_recv()
            total = total + rrecv[d, m * CHUNK : (m + 1) * CHUNK, :].astype(F32)
        ot[part * CHUNK : (part + 1) * CHUNK, :] = (scale * total).astype(BF16)
        outs.append(pltpu.make_async_copy(ot.at[rows], gt_out.at[0, rows], out_sem.at[1 + part]))
        outs[-1].start()
    for copy in started:
        copy.wait_send()
    for copy in (*z_img, *back, *z_own):
        copy.wait_send()

    @pl.when(has_next)
    def _():
        for copy in next_own + next_other:
            copy.wait_send()

    @pl.when(inlet)
    def _():
        for copy in passed[2] + passed[3]:
            copy.wait_send()

    for copy in outs:
        copy.wait()


def body(image, text, logit_scale, lse_row, lse_col, pair):
    width = image.shape[2]
    msgs = 3 * PARTS + PARTS // 2
    hbm = pl.BlockSpec(memory_space=pltpu.HBM)
    dma = pltpu.SemaphoreType.DMA
    out = jax.ShapeDtypeStruct((1, ROWS, width), BF16)
    return pl.pallas_call(
        kernel,
        out_shape=(out, out),
        in_specs=[hbm, hbm, pl.BlockSpec(memory_space=pltpu.SMEM), hbm, hbm, hbm],
        out_specs=(hbm, hbm),
        scratch_shapes=[
            pltpu.VMEM((PLACES * ROWS, width), BF16),
            pltpu.VMEM((4 * ROWS, width), BF16),
            pltpu.VMEM((4, 8, ROWS), F32),
            pltpu.VMEM((PLACES, 8, ROWS), F32),
            pltpu.VMEM((PLACES * ROWS, ROWS), F32),
            pltpu.VMEM((PLACES * ROWS, 4 * ROWS), BF16),
            pltpu.VMEM((PLACES * ROWS, width), F32),
            pltpu.VMEM((2, msgs * CHUNK, width), BF16),
            pltpu.VMEM((2, msgs * CHUNK, width), BF16),
            pltpu.VMEM((2 * ROWS, width), F32),
            pltpu.VMEM((2 * ROWS, width), F32),
            pltpu.VMEM((2 * ROWS, width), BF16),
            pltpu.VMEM((4 * ROWS, width), BF16),
            pltpu.VMEM((ROWS, width), BF16),
            pltpu.VMEM((ROWS, width), BF16),
            pltpu.VMEM((2, 1, ROWS), BF16),
            pltpu.VMEM((1, ROWS), jnp.int32),
            pltpu.VMEM((ROWS, width), BF16),
            pltpu.VMEM((ROWS, width), BF16),
            dma((5,)),
            dma((1 + PARTS,)),
            dma((2, msgs)),
            dma((2, msgs)),
            dma((2, msgs)),
            dma((2, msgs)),
            dma((10,)),
            dma((6,)),
            dma((5,)),
            dma((3,)),
            dma((2, 4)),
            dma((2, 4)),
            dma((4,)),
            dma((8,)),
            dma((2,)),
            dma((2,)),
        ],
        compiler_params=pltpu.CompilerParams(
            collective_id=0, has_side_effects=True, vmem_limit_bytes=63 * 2**20
        ),
        cost_estimate=pl.CostEstimate(
            flops=12 * ROWS * 16 * ROWS * width, bytes_accessed=8 * ROWS * width, transcendentals=8 * ROWS * 16 * ROWS
        ),
    )(image, text, jnp.reshape(logit_scale, (1,)), lse_row, lse_col, pair)


def solution(mesh):
    return jax.shard_map(
        body,
        mesh=mesh,
        in_specs=(
            P("blk", "grp", None),
            P("blk", "grp", None),
            P(),
            P("blk", "grp"),
            P("blk", "grp"),
            P("blk", "grp"),
        ),
        out_specs=(P("blk", "grp", None), P("blk", "grp", None)),
        check_vma=False,
    )
```

```python
import functools

import jax
import jax.numpy as jnp
from jax import lax
from jax.experimental import pallas as pl
from jax.experimental.pallas import tpu as pltpu
from jax.sharding import PartitionSpec as P

MESH = pl.DeviceIdType.MESH
RING = 8
ROWS = 128
PARTS = 4
STEP = PARTS // 4
CHUNK = ROWS // PARTS
HALF = ROWS // 2
PLACES = 8
RUN = 8
FAR = ((2, 3), (1, 0))
F32 = jnp.float32
BF16 = jnp.bfloat16


def place(direction, hops):
    return 0 if hops == 0 else 7 if hops == 4 else 2 * hops - 1 + direction


def gather_order(direction):
    far, near = FAR[direction], FAR[1 - direction]
    order = [(hop, part) for hop in (1, 2, 3) for part in far + near]
    return order + [(4, part) for part in far]


def reduce_order(direction):
    f0, f1 = FAR[direction][:STEP], FAR[direction][STEP:]
    n0, n1 = FAR[1 - direction][:STEP], FAR[1 - direction][STEP:]
    order = [
        (3, n0), (3, n1), (4, f0), (4, f1), (2, n0), (3, f0), (3, f1),
        (2, n1), (2, f0), (2, f1), (1, n0), (1, f0), (1, f1), (1, n1),
    ]
    return [(hops, part) for hops, parts in order for part in parts]


def kernel(
    image, text, scale_ref, lrow_ref, lcol_ref, pair_ref, gi_out, gt_out,
    txt, img, imgt, meta, col, lct, dt, ct, rsend, rrecv, g0, g1, gis, gir, zs, zr, vecs, pairs,
    local_sem, ag_s, rs_s, ring_r, im_s, im_r, me_s, me_r, co_s, co_r, gi_s, gi_r, zz_s, zz_r,
):
    g = lax.axis_index("grp")
    b = lax.axis_index("blk")
    n_blk = lax.axis_size("blk")
    n_grp = 2 * RING
    zpart = g + 1 - 2 * lax.rem(g, 2)
    nxt = lax.rem(b + 1, n_blk)
    prv = lax.rem(b + n_blk - 1, n_blk)
    ring = [lax.rem(g + 2 * i, n_grp) for i in range(RING)]
    side = [ring[1], ring[7]]
    z_lo = lax.rem(g, 2)
    last = lax.rem(b, RUN) == RUN - 1
    first = lax.rem(b, RUN) == 0
    zero = b == 0
    has_next = jnp.logical_not(jnp.logical_and(last, z_lo == 0))
    has_prev = jnp.logical_not(jnp.logical_and(first, z_lo == 1))
    outlet = jnp.logical_and(last, z_lo == 1)
    inlet = jnp.logical_and(first, z_lo == 0)
    next_grp = jnp.where(last, zpart, g)
    prev_grp = jnp.where(first, zpart, g)

    barrier = pltpu.get_barrier_semaphore()

    def greet(grp, blk):
        pl.semaphore_signal(barrier, inc=1, device_id={"grp": grp, "blk": blk}, device_id_type=MESH)

    greet(side[0], b)
    greet(side[1], b)
    greet(zpart, b)

    @pl.when(has_prev)
    def _():
        greet(prev_grp, prv)

    def copy_to(src, dst, s_sem, r_sem, grp=g, blk=b):
        return pltpu.make_async_remote_copy(
            src_ref=src, dst_ref=dst, send_sem=s_sem, recv_sem=r_sem,
            device_id={"grp": grp, "blk": blk}, device_id_type=MESH,
        )

    local = [
        pltpu.make_async_copy(src, dst, local_sem.at[i])
        for i, (src, dst) in enumerate((
            (pair_ref, pairs),
            (lrow_ref, vecs.at[0]),
            (lcol_ref, vecs.at[1]),
            (text.at[0], txt.at[pl.ds(0, ROWS)]),
            (image.at[0], img.at[pl.ds(0, ROWS)]),
        ))
    ]
    for copy in local:
        copy.start()
    scale = scale_ref[0]

    def go(copy):
        copy.start()

    orders = [gather_order(0), gather_order(1)]

    def gather_copy(direction, n):
        hop, part = orders[direction][n]
        rows = lambda p: txt.at[pl.ds(p * ROWS + part * CHUNK, CHUNK)]
        src = text.at[0, pl.ds(part * CHUNK, CHUNK)] if hop == 1 else rows(place(direction, hop - 1))
        return copy_to(
            src, rows(place(direction, hop)), ag_s, ring_r.at[direction, n], grp=side[direction]
        )

    def col_copy(direction, hop):
        return copy_to(
            col.at[place(direction, hop - 1)], col.at[place(direction, hop)],
            co_s, co_r.at[direction, hop - 1], grp=side[direction],
        )

    gather = [[gather_copy(d, n) for n in range(len(orders[d]))] for d in range(2)]
    cols = [[col_copy(0, hop) for hop in (1, 2, 3, 4)], [col_copy(1, hop) for hop in (1, 2, 3)]]

    def arrived(*steps):
        for n in [STEP * step + i for step in steps for i in range(STEP)]:
            hop = n // PARTS + 1
            for d in range(2):
                gather[d][n].wait_recv()
                if n + PARTS < len(orders[d]):
                    go(gather[d][n + PARTS])
            for d in range(2):
                if n % PARTS == (PARTS // 2 if hop < 4 else 0) and hop <= len(cols[d]):
                    cols[d][hop - 1].wait_recv()
                    if hop < len(cols[d]):
                        go(cols[d][hop])

    def image_copies(src, dst, sem, **to):
        def copy(i):
            start = i * HALF
            rows = image.at[0, pl.ds(start, HALF)] if src == 0 else img.at[pl.ds(src * ROWS + start, HALF)]
            r_sem = im_r.at[2 * (dst - 1) + i]
            return copy_to(rows, img.at[pl.ds(dst * ROWS + start, HALF)], im_s.at[sem], r_sem, **to)

        return copy(0), copy(1), copy_to(meta.at[src], meta.at[dst], me_s.at[sem], me_r.at[dst - 1], **to)

    swap = last.astype(jnp.int32)
    z_img = image_copies(0, 1, 0, grp=zpart)
    next_own = image_copies(0, 2 + swap, 1, grp=next_grp, blk=nxt)
    next_other = image_copies(1, 3 - swap, 2, grp=next_grp, blk=nxt)
    passed = {3: image_copies(3, 2, 3, grp=zpart), 2: image_copies(2, 3, 4, grp=zpart)}
    arrivals = {2: image_copies(0, 2, 0, grp=zpart), 3: image_copies(0, 3, 0, grp=zpart)}

    def image_arrived(slot):
        for copy in arrivals[slot]:
            copy.wait_recv()

    def start_if(condition, copies):
        @pl.when(condition)
        def _():
            for copy in copies:
                copy.start()

    def pass_on(condition, slot):
        @pl.when(condition)
        def _():
            for got, copy in zip(arrivals[slot], passed[slot]):
                got.wait_recv()
                copy.start()

    def take(ref, parts):
        pieces = []
        for p, part in parts:
            lo = p * ROWS + part * CHUNK
            if pieces and pieces[-1][1] == lo:
                pieces[-1][1] = lo + CHUNK
            else:
                pieces.append([lo, lo + CHUNK])
        pieces = [ref[lo:hi, :] for lo, hi in pieces]
        return pieces[0] if len(pieces) == 1 else jnp.concatenate(pieces, axis=0)

    def whole(*places):
        return [(p, part) for p in places for part in range(PARTS)]

    def columns(*places):
        for p in places:
            lct[p * ROWS : (p + 1) * ROWS, :] = jnp.broadcast_to(col[p, 0:1, :], (ROWS, ROWS)).T

    def turn(slot):
        imgt[:, slot * ROWS : (slot + 1) * ROWS] = img[slot * ROWS : (slot + 1) * ROWS, :].T

    def scores(parts):
        s = jnp.dot(take(txt, parts), imgt[...], preferred_element_type=F32) * scale
        lr = jnp.concatenate([meta[slot, 0:1, :] for slot in range(4)], axis=1)
        lc = take(lct, parts)
        d = 0.5 * (jnp.exp(s - lr) + jnp.exp(s - jnp.concatenate([lc] * 4, axis=1)))
        pr = jnp.concatenate([meta[0, 1:2, :], meta[1, 1:2, :]], axis=1).astype(jnp.int32)
        iota = lax.broadcasted_iota(jnp.int32, (CHUNK, 2 * ROWS), 0)
        for i, (p, part) in enumerate(parts):
            rel = 0 if p == 0 else 4 if p == 7 else (RING - (p + 1) // 2) if p % 2 else p // 2
            rows = d[i * CHUNK : (i + 1) * CHUNK]
            own = rows[:, : 2 * ROWS] - (pr - (ring[rel] * ROWS + part * CHUNK) == iota).astype(F32)
            lo = p * ROWS + part * CHUNK
            dt[lo : lo + CHUNK, : 2 * ROWS] = own.astype(BF16)
            dt[lo : lo + CHUNK, 2 * ROWS :] = rows[:, 2 * ROWS :].astype(BF16)

    def contribution(parts):
        c = jnp.dot(take(dt, parts), img[...], preferred_element_type=F32)
        for i, (p, part) in enumerate(parts):
            lo = p * ROWS + part * CHUNK
            ct[lo : lo + CHUNK, :] = c[i * CHUNK : (i + 1) * CHUNK]

    def image_term(k):
        return lax.dot_general(
            dt[:, k * 2 * ROWS : (k + 1) * 2 * ROWS], txt[...], (((0,), (0,)), ((), ())), preferred_element_type=F32
        )

    r_orders = [reduce_order(0), reduce_order(1)]

    def reduce_copy(direction, n):
        rows = pl.ds(n * CHUNK, CHUNK)
        return copy_to(
            rsend.at[direction, rows], rrecv.at[direction, rows],
            rs_s, ring_r.at[direction, n], grp=side[direction],
        )

    reduction = [[reduce_copy(d, n) for n in range(len(r_orders[d]))] for d in range(2)]

    def reduce_step(*steps):
        for n in [STEP * step + i for step in steps for i in range(STEP)]:
            for d in range(2):
                hops, part = r_orders[d][n]
                start = place(1 - d, hops) * ROWS + part * CHUNK
                total = ct[start : start + CHUNK, :]
                if (hops + 1, part) in r_orders[d]:
                    m = r_orders[d].index((hops + 1, part))
                    reduction[d][m].wait_recv()
                    total = total + rrecv[d, m * CHUNK : (m + 1) * CHUNK, :].astype(F32)
                rsend[d, n * CHUNK : (n + 1) * CHUNK, :] = total.astype(BF16)
                go(reduction[d][n])

    half = lambda j: slice(j * HALF, (j + 1) * HALF)
    feeder = jnp.logical_and(first, z_lo == 1)
    back_blk = jnp.where(feeder, b, prv)

    def back_copy(j):
        if j < 2:
            to = jnp.where(feeder, j + 6, jnp.where(inlet, j + 2, j))
        else:
            to = jnp.where(feeder, j + 2, jnp.where(inlet, j - 2, j))
        return copy_to(
            gis.at[pl.ds(j * HALF, HALF)], gir.at[pl.ds(pl.multiple_of(to * HALF, HALF), HALF)],
            gi_s, gi_r.at[to], grp=prev_grp, blk=back_blk,
        )

    back = [back_copy(j) for j in range(4)]

    def back_wait(to):
        rows = pl.ds(to * HALF, HALF)
        copy_to(gis.at[pl.ds(0, HALF)], gir.at[rows], gi_s, gi_r.at[to], grp=zpart).wait_recv()

    def inlet_back(j):
        @pl.when(inlet)
        def _():
            back_wait(4 + j)
            gis[half(j), :] = (g1[half(j), :] + gir[half(4 + j), :].astype(F32)).astype(BF16)
            back[j].start()

    z_own = [
        copy_to(zs.at[pl.ds(i * HALF, HALF)], zr.at[pl.ds(i * HALF, HALF)], zz_s, zz_r.at[i], grp=zpart)
        for i in range(2)
    ]

    def own_back(condition):
        @pl.when(condition)
        def _():
            for i in range(2):

                @pl.when(has_next)
                def _():
                    back_wait(2 + i)

                zs[half(i), :] = (g0[half(2 + i), :] + gir[half(2 + i), :].astype(F32)).astype(BF16)
                z_own[i].start()

    pl.semaphore_wait(barrier, 3 + has_next.astype(jnp.int32))
    for n in range(PARTS):
        for d in range(2):
            go(gather[d][n])
    start_if(True, z_img[:2])
    start_if(has_next, next_own[:2])
    for copy in local[:3]:
        copy.wait()
    meta[0] = jnp.zeros((8, ROWS), F32)
    meta[0, 0:1, :] = vecs[0].astype(F32)
    meta[0, 1:2, :] = pairs[...].astype(F32)
    col[0] = jnp.broadcast_to(vecs[1].astype(F32), (8, ROWS))
    start_if(True, z_img[2:])
    start_if(has_next, next_own[2:])
    for d in range(2):
        go(cols[d][0])
    for copy in local[3:]:
        copy.wait()
    columns(0)
    arrived(0, 1)

    @pl.when(outlet)
    def _():
        for got, copy in zip(z_img, next_other):
            got.wait_recv()
            copy.start()

    arrived(2)
    pass_on(jnp.logical_and(inlet, jnp.logical_not(zero)), 3)
    arrived(3)

    @pl.when(jnp.logical_not(outlet))
    def _():
        for copy in z_img:
            copy.wait_recv()

    start_if(jnp.logical_not(last), next_other)
    turn(0)
    turn(1)
    columns(1, 2)
    arrived(4)
    pass_on(jnp.logical_and(inlet, jnp.logical_not(zero)), 2)
    arrived(5, 6, 7)
    pass_on(jnp.logical_and(inlet, zero), 3)
    columns(3, 4)
    arrived(8, 9)
    pass_on(jnp.logical_and(inlet, zero), 2)
    near = sorted([(5, part) for part in FAR[0]] + [(6, part) for part in FAR[1]])
    far = sorted([(5, part) for part in FAR[1]] + [(6, part) for part in FAR[0]])

    @pl.when(jnp.logical_not(inlet))
    def _():
        image_arrived(2)
        image_arrived(3)

    turn(2)
    turn(3)
    arrived(10)
    columns(5, 6)
    scores(near)
    contribution(near)
    reduce_step(0, 1)
    scores(whole(0, 1, 2, 3, 4))
    arrived(11)
    scores(far)
    arrived(12)
    columns(7)
    opposite = sorted((7, part) for d in range(2) for part in FAR[d][:STEP])
    scores(opposite)
    contribution(opposite)
    reduce_step(2)
    arrived(13)
    opposite = sorted((7, part) for d in range(2) for part in FAR[d][STEP:])
    scores(opposite)
    contribution(opposite)
    reduce_step(3)
    g1[...] = image_term(1)

    @pl.when(jnp.logical_not(inlet))
    def _():
        for j in (2, 3, 0, 1):
            gis[half(j), :] = g1[half(j), :].astype(BF16)
            back[j].start()

    @pl.when(jnp.logical_not(has_next))
    def _():
        gir[0 : 2 * ROWS, :] = jnp.zeros((2 * ROWS, gir.shape[1]), BF16)

    contribution(whole(3, 4))
    reduce_step(4)
    contribution(far)
    reduce_step(5, 6)
    contribution(whole(1, 2))
    g0[...] = image_term(0)
    contribution(whole(0))
    reduce_step(7, 8)
    own_back(jnp.logical_not(last))
    inlet_back(0)
    reduce_step(9)
    inlet_back(1)
    reduce_step(10)
    inlet_back(2)
    reduce_step(11)
    inlet_back(3)
    reduce_step(12, 13)
    own_back(last)

    @pl.when(has_next)
    def _():
        back_wait(0)
        back_wait(1)

    for copy in z_own:
        copy.wait_recv()
    gi_out[0] = (scale * (g0[:ROWS, :] + gir[:ROWS, :].astype(F32) + zr[...].astype(F32))).astype(BF16)
    for part in sorted(range(PARTS), key=lambda part: r_orders[0].index((1, part)) + r_orders[1].index((1, part))):
        total = ct[part * CHUNK : (part + 1) * CHUNK, :]
        for d in range(2):
            m = r_orders[d].index((1, part))
            reduction[d][m].wait_recv()
            total = total + rrecv[d, m * CHUNK : (m + 1) * CHUNK, :].astype(F32)
        gt_out[0, part * CHUNK : (part + 1) * CHUNK, :] = (scale * total).astype(BF16)

    def all_sent(ref, sem):
        pltpu.make_async_copy(ref, ref, sem).wait()

    def images_sent(*sems):
        for sem in sems:
            all_sent(img.at[pl.ds(0, ROWS)], im_s.at[sem])
            all_sent(meta.at[0], me_s.at[sem])

    all_sent(rrecv, ag_s)
    all_sent(rrecv, rs_s)
    all_sent(col.at[pl.ds(0, 7)], co_s)
    all_sent(gis, gi_s)
    all_sent(zs, zz_s)
    images_sent(0)

    @pl.when(has_next)
    def _():
        images_sent(1, 2)

    @pl.when(inlet)
    def _():
        images_sent(3, 4)


def write(gi, gt, gi_out, gt_out, sems):
    copies = [pltpu.make_async_copy(src, dst, sems.at[i]) for i, (src, dst) in enumerate(((gi, gi_out), (gt, gt_out)))]
    for copy in copies:
        copy.start()
    for copy in copies:
        copy.wait()


def body(image, text, logit_scale, lse_row, lse_col, pair):
    width = image.shape[2]
    msgs = 3 * PARTS + PARTS // 2
    hbm = pl.BlockSpec(memory_space=pltpu.HBM)
    dma = pltpu.SemaphoreType.DMA
    vmem = pl.BlockSpec(memory_space=pltpu.VMEM)
    out = pltpu.VMEM((1, ROWS, width), BF16)
    grads = pl.pallas_call(
        kernel,
        out_shape=(out, out),
        in_specs=[hbm, hbm, pl.BlockSpec(memory_space=pltpu.SMEM), hbm, hbm, hbm],
        out_specs=(vmem, vmem),
        scratch_shapes=[
            pltpu.VMEM((PLACES * ROWS, width), BF16),
            pltpu.VMEM((4 * ROWS, width), BF16),
            pltpu.VMEM((width, 4 * ROWS), BF16),
            pltpu.VMEM((4, 8, ROWS), F32),
            pltpu.VMEM((PLACES, 8, ROWS), F32),
            pltpu.VMEM((PLACES * ROWS, ROWS), F32),
            pltpu.VMEM((PLACES * ROWS, 4 * ROWS), BF16),
            pltpu.VMEM((PLACES * ROWS, width), F32),
            pltpu.VMEM((2, msgs * CHUNK, width), BF16),
            pltpu.VMEM((2, msgs * CHUNK, width), BF16),
            pltpu.VMEM((2 * ROWS, width), F32),
            pltpu.VMEM((2 * ROWS, width), F32),
            pltpu.VMEM((2 * ROWS, width), BF16),
            pltpu.VMEM((4 * ROWS, width), BF16),
            pltpu.VMEM((ROWS, width), BF16),
            pltpu.VMEM((ROWS, width), BF16),
            pltpu.VMEM((2, 1, ROWS), BF16),
            pltpu.VMEM((1, ROWS), jnp.int32),
            dma((5,)),
            dma,
            dma,
            dma((2, msgs)),
            dma((5,)),
            dma((6,)),
            dma((5,)),
            dma((3,)),
            dma,
            dma((2, 4)),
            dma,
            dma((8,)),
            dma,
            dma((2,)),
        ],
        compiler_params=pltpu.CompilerParams(
            collective_id=0, has_side_effects=True, vmem_limit_bytes=63 * 2**20
        ),
        cost_estimate=pl.CostEstimate(
            flops=12 * ROWS * 16 * ROWS * width, bytes_accessed=8 * ROWS * width, transcendentals=8 * ROWS * 16 * ROWS
        ),
    )(image, text, jnp.reshape(logit_scale, (1,)), lse_row, lse_col, pair)
    return pl.pallas_call(
        write,
        out_shape=[jax.ShapeDtypeStruct((1, ROWS, width), BF16)] * 2,
        in_specs=[vmem, vmem],
        out_specs=[hbm, hbm],
        scratch_shapes=[dma((2,))],
        compiler_params=pltpu.CompilerParams(vmem_limit_bytes=2**20),
    )(*grads)


def solution(mesh):
    return jax.shard_map(
        body,
        mesh=mesh,
        in_specs=(
            P("blk", "grp", None),
            P("blk", "grp", None),
            P(),
            P("blk", "grp"),
            P("blk", "grp"),
            P("blk", "grp"),
        ),
        out_specs=(P("blk", "grp", None), P("blk", "grp", None)),
        check_vma=False,
    )
```

```python
import functools

import jax
import jax.numpy as jnp
from jax import lax
from jax.experimental import pallas as pl
from jax.experimental.pallas import tpu as pltpu
from jax.sharding import PartitionSpec as P

MESH = pl.DeviceIdType.MESH
RING = 8
ROWS = 128
PARTS = 4
STEP = PARTS // 4
CHUNK = ROWS // PARTS
HALF = ROWS // 2
PLACES = 8
RUN = 8
FAR = ((2, 3), (1, 0))
F32 = jnp.float32
BF16 = jnp.bfloat16


def place(direction, hops):
    return 0 if hops == 0 else 7 if hops == 4 else 2 * hops - 1 + direction


def gather_order(direction):
    far, near = FAR[direction], FAR[1 - direction]
    order = [(hop, part) for hop in (1, 2, 3) for part in far + near]
    return order + [(4, part) for part in far]


def reduce_order(direction):
    f0, f1 = FAR[direction][:STEP], FAR[direction][STEP:]
    n0, n1 = FAR[1 - direction][:STEP], FAR[1 - direction][STEP:]
    order = [
        (3, n0), (3, n1), (4, f0), (4, f1), (2, n0), (3, f0), (3, f1),
        (2, n1), (2, f0), (2, f1), (1, n0), (1, f0), (1, f1), (1, n1),
    ]
    return [(hops, part) for hops, parts in order for part in parts]


def kernel(
    image, text, scale_ref, lrow_ref, lcol_ref, pair_ref, gi_out, gt_out,
    txt, img, imgt, meta, col, lct, dt, ct, rsend, rrecv, g0, g1, gis, gir, zs, zr, vecs, pairs,
    ready, local_sem, ag_s, rs_s, ring_r, im_s, im_r, me_s, me_r, co_s, co_r, gi_s, gi_r, zz_s, zz_r,
):
    g = lax.axis_index("grp")
    b = lax.axis_index("blk")
    n_blk = lax.axis_size("blk")
    n_grp = 2 * RING
    zpart = g + 1 - 2 * lax.rem(g, 2)
    nxt = lax.rem(b + 1, n_blk)
    prv = lax.rem(b + n_blk - 1, n_blk)
    ring = [lax.rem(g + 2 * i, n_grp) for i in range(RING)]
    side = [ring[1], ring[7]]
    z_lo = lax.rem(g, 2)
    last = lax.rem(b, RUN) == RUN - 1
    first = lax.rem(b, RUN) == 0
    zero = b == 0
    low, high = z_lo == 0, z_lo == 1
    no = jnp.logical_not
    both = jnp.logical_and
    has_next = no(both(last, low))
    has_prev = no(both(first, high))
    outlet = both(last, high)
    inlet = both(first, low)
    next_grp = jnp.where(last, zpart, g)
    prev_grp = jnp.where(first, zpart, g)

    y = g // 2
    origin = both(zero, low)
    left_first = jnp.where(y == 0, origin, both(y < 7, no(both(origin, y == 1))))
    right_first = jnp.where(y == 0, origin, jnp.where(y == 7, no(origin), y == 6))
    z_first = jnp.where(both(zero, y == 0), low, high)
    prev_first = both(has_prev, no(zero))
    next_first = both(has_next, nxt == 0)
    meets = (
        (left_first, True, side[1], b, 1),
        (right_first, True, side[0], b, 0),
        (z_first, True, zpart, b, 2),
        (prev_first, has_prev, prev_grp, prv, 3),
        (next_first, has_next, next_grp, nxt, None),
    )
    barrier = pltpu.get_barrier_semaphore()

    def greet(grp, blk, sem):
        pl.semaphore_signal(sem, inc=1, device_id={"grp": grp, "blk": blk}, device_id_type=MESH)

    for they_first, met, grp, blk, _ in meets:

        @pl.when(both(met, no(they_first)))
        def _(grp=grp, blk=blk):
            greet(grp, blk, barrier)

    def copy_to(src, dst, s_sem, r_sem, grp=g, blk=b):
        return pltpu.make_async_remote_copy(
            src_ref=src, dst_ref=dst, send_sem=s_sem, recv_sem=r_sem,
            device_id={"grp": grp, "blk": blk}, device_id_type=MESH,
        )

    local = [
        pltpu.make_async_copy(src, dst, local_sem.at[i])
        for i, (src, dst) in enumerate((
            (pair_ref, pairs),
            (lrow_ref, vecs.at[0]),
            (lcol_ref, vecs.at[1]),
            (text.at[0], txt.at[pl.ds(0, ROWS)]),
            (image.at[0], img.at[pl.ds(0, ROWS)]),
        ))
    ]
    for copy in local:
        copy.start()
    scale = scale_ref[0]

    def go(copy):
        copy.start()

    orders = [gather_order(0), gather_order(1)]

    def gather_copy(direction, n):
        hop, part = orders[direction][n]
        rows = lambda p: txt.at[pl.ds(p * ROWS + part * CHUNK, CHUNK)]
        src = text.at[0, pl.ds(part * CHUNK, CHUNK)] if hop == 1 else rows(place(direction, hop - 1))
        return copy_to(
            src, rows(place(direction, hop)), ag_s, ring_r.at[direction, n], grp=side[direction]
        )

    def col_copy(direction, hop):
        return copy_to(
            col.at[place(direction, hop - 1)], col.at[place(direction, hop)],
            co_s, co_r.at[direction, hop - 1], grp=side[direction],
        )

    gather = [[gather_copy(d, n) for n in range(len(orders[d]))] for d in range(2)]
    cols = [[col_copy(0, hop) for hop in (1, 2, 3, 4)], [col_copy(1, hop) for hop in (1, 2, 3)]]

    def arrived(*steps):
        for n in [STEP * step + i for step in steps for i in range(STEP)]:
            hop = n // PARTS + 1
            for d in range(2):
                if n % PARTS == 0 and hop <= len(cols[d]):
                    cols[d][hop - 1].wait_recv()
                    if hop < len(cols[d]):
                        go(cols[d][hop])
                gather[d][n].wait_recv()
                if n + PARTS < len(orders[d]):
                    go(gather[d][n + PARTS])

    def image_copies(src, dst, sem, **to):
        def copy(i):
            start = i * HALF
            rows = image.at[0, pl.ds(start, HALF)] if src == 0 else img.at[pl.ds(src * ROWS + start, HALF)]
            r_sem = im_r.at[2 * (dst - 1) + i]
            return copy_to(rows, img.at[pl.ds(dst * ROWS + start, HALF)], im_s.at[sem], r_sem, **to)

        return copy(0), copy(1), copy_to(meta.at[src], meta.at[dst], me_s.at[sem], me_r.at[dst - 1], **to)

    swap = last.astype(jnp.int32)
    z_img = image_copies(0, 1, 0, grp=zpart)
    next_own = image_copies(0, 2 + swap, 1, grp=next_grp, blk=nxt)
    next_other = image_copies(1, 3 - swap, 2, grp=next_grp, blk=nxt)
    passed = {3: image_copies(3, 2, 3, grp=zpart), 2: image_copies(2, 3, 4, grp=zpart)}
    arrivals = {2: image_copies(0, 2, 0, grp=zpart), 3: image_copies(0, 3, 0, grp=zpart)}

    def image_arrived(slot):
        for copy in arrivals[slot]:
            copy.wait_recv()

    def start_if(condition, copies):
        @pl.when(condition)
        def _():
            for copy in copies:
                copy.start()

    def pass_on(condition, slot):
        @pl.when(condition)
        def _():
            for got, copy in zip(arrivals[slot], passed[slot]):
                got.wait_recv()
                copy.start()

    def take(ref, parts):
        pieces = []
        for p, part in parts:
            lo = p * ROWS + part * CHUNK
            if pieces and pieces[-1][1] == lo:
                pieces[-1][1] = lo + CHUNK
            else:
                pieces.append([lo, lo + CHUNK])
        pieces = [ref[lo:hi, :] for lo, hi in pieces]
        return pieces[0] if len(pieces) == 1 else jnp.concatenate(pieces, axis=0)

    def whole(*places):
        return [(p, part) for p in places for part in range(PARTS)]

    def columns(*places):
        for p in places:
            lct[p * ROWS : (p + 1) * ROWS, :] = jnp.broadcast_to(col[p, 0:1, :], (ROWS, ROWS)).T

    def turn(slot):
        imgt[:, slot * ROWS : (slot + 1) * ROWS] = img[slot * ROWS : (slot + 1) * ROWS, :].T

    def scores(parts):
        s = jnp.dot(take(txt, parts), imgt[...], preferred_element_type=F32) * scale
        lr = jnp.concatenate([meta[slot, 0:1, :] for slot in range(4)], axis=1)
        lc = take(lct, parts)
        d = 0.5 * (jnp.exp(s - lr) + jnp.exp(s - jnp.concatenate([lc] * 4, axis=1)))
        pr = jnp.concatenate([meta[0, 1:2, :], meta[1, 1:2, :]], axis=1).astype(jnp.int32)
        iota = lax.broadcasted_iota(jnp.int32, (CHUNK, 2 * ROWS), 0)
        for i, (p, part) in enumerate(parts):
            rel = 0 if p == 0 else 4 if p == 7 else (RING - (p + 1) // 2) if p % 2 else p // 2
            rows = d[i * CHUNK : (i + 1) * CHUNK]
            own = rows[:, : 2 * ROWS] - (pr - (ring[rel] * ROWS + part * CHUNK) == iota).astype(F32)
            lo = p * ROWS + part * CHUNK
            dt[lo : lo + CHUNK, : 2 * ROWS] = own.astype(BF16)
            dt[lo : lo + CHUNK, 2 * ROWS :] = rows[:, 2 * ROWS :].astype(BF16)

    def contribution(parts):
        c = jnp.dot(take(dt, parts), img[...], preferred_element_type=F32)
        for i, (p, part) in enumerate(parts):
            lo = p * ROWS + part * CHUNK
            ct[lo : lo + CHUNK, :] = c[i * CHUNK : (i + 1) * CHUNK]

    def image_term(k):
        return lax.dot_general(
            dt[:, k * 2 * ROWS : (k + 1) * 2 * ROWS], txt[...], (((0,), (0,)), ((), ())), preferred_element_type=F32
        )

    r_orders = [reduce_order(0), reduce_order(1)]

    def reduce_copy(direction, n):
        rows = pl.ds(n * CHUNK, CHUNK)
        return copy_to(
            rsend.at[direction, rows], rrecv.at[direction, rows],
            rs_s, ring_r.at[direction, n], grp=side[direction],
        )

    reduction = [[reduce_copy(d, n) for n in range(len(r_orders[d]))] for d in range(2)]

    def reduce_step(*steps):
        for n in [STEP * step + i for step in steps for i in range(STEP)]:
            for d in range(2):
                hops, part = r_orders[d][n]
                start = place(1 - d, hops) * ROWS + part * CHUNK
                total = ct[start : start + CHUNK, :]
                if (hops + 1, part) in r_orders[d]:
                    m = r_orders[d].index((hops + 1, part))
                    reduction[d][m].wait_recv()
                    total = total + rrecv[d, m * CHUNK : (m + 1) * CHUNK, :].astype(F32)
                rsend[d, n * CHUNK : (n + 1) * CHUNK, :] = total.astype(BF16)
                go(reduction[d][n])

    half = lambda j: slice(j * HALF, (j + 1) * HALF)
    feeder = jnp.logical_and(first, z_lo == 1)
    back_blk = jnp.where(feeder, b, prv)

    def back_copy(j):
        if j < 2:
            to = jnp.where(feeder, j + 6, jnp.where(inlet, j + 2, j))
        else:
            to = jnp.where(feeder, j + 2, jnp.where(inlet, j - 2, j))
        return copy_to(
            gis.at[pl.ds(j * HALF, HALF)], gir.at[pl.ds(pl.multiple_of(to * HALF, HALF), HALF)],
            gi_s, gi_r.at[to], grp=prev_grp, blk=back_blk,
        )

    back = [back_copy(j) for j in range(4)]

    def back_wait(to):
        rows = pl.ds(to * HALF, HALF)
        copy_to(gis.at[pl.ds(0, HALF)], gir.at[rows], gi_s, gi_r.at[to], grp=zpart).wait_recv()

    def inlet_back(condition, j):
        @pl.when(both(inlet, condition))
        def _():
            back_wait(4 + j)
            gis[half(j), :] = (g1[half(j), :] + gir[half(4 + j), :].astype(F32)).astype(BF16)
            back[j].start()

    z_own = [
        copy_to(zs.at[pl.ds(i * HALF, HALF)], zr.at[pl.ds(i * HALF, HALF)], zz_s, zz_r.at[i], grp=zpart)
        for i in range(2)
    ]

    def own_back(condition, *halves):
        @pl.when(condition)
        def _():
            for i in halves:

                @pl.when(has_next)
                def _():
                    back_wait(2 + i)

                zs[half(i), :] = (g0[half(2 + i), :] + gir[half(2 + i), :].astype(F32)).astype(BF16)
                z_own[i].start()

    for copy in local[:3]:
        copy.wait()
    meta[0] = jnp.zeros((8, ROWS), F32)
    meta[0, 0:1, :] = vecs[0].astype(F32)
    meta[0, 1:2, :] = pairs[...].astype(F32)
    col[0] = jnp.broadcast_to(vecs[1].astype(F32), (8, ROWS))
    greeted = sum(they_first.astype(jnp.int32) for they_first, _, _, _, _ in meets)

    @pl.when(greeted > 0)
    def _():
        pl.semaphore_wait(barrier, greeted)

    for they_first, _, grp, blk, sem in meets:
        if sem is not None:

            @pl.when(they_first)
            def _(grp=grp, blk=blk, sem=sem):
                greet(grp, blk, ready.at[sem])

    def open_side(condition, d, answer):
        @pl.when(condition)
        def _():
            if answer:
                pl.semaphore_wait(ready.at[1 - d], 1)
            cols[d][0].start()
            for n in range(PARTS):
                gather[d][n].start()

    open_side(left_first, 1, False)
    open_side(right_first, 0, False)
    open_side(no(right_first), 0, True)
    open_side(no(left_first), 1, True)
    beside = lax.rem(b, RUN) == RUN - 2
    held = jnp.logical_or(beside, both(both(zero, y == 0), high))

    def open_z(condition):
        @pl.when(condition)
        def _():
            @pl.when(no(z_first))
            def _():
                pl.semaphore_wait(ready.at[2], 1)

            for copy in z_img:
                copy.start()

    open_z(no(held))

    @pl.when(has_next)
    def _():
        @pl.when(no(next_first))
        def _():
            pl.semaphore_wait(ready.at[3], 1)

        for copy in next_own:
            copy.start()

    for copy in local[3:]:
        copy.wait()
    columns(0)
    arrived(0)

    @pl.when(outlet)
    def _():
        z_img[0].wait_recv()
        next_other[0].start()

    arrived(1)
    open_z(held)

    @pl.when(outlet)
    def _():
        for got, copy in zip(z_img[1:], next_other[1:]):
            got.wait_recv()
            copy.start()

    arrived(2)
    pass_on(both(inlet, no(zero)), 3)
    arrived(3)

    def z_arrived(condition):
        @pl.when(condition)
        def _():
            for copy in z_img:
                copy.wait_recv()

            @pl.when(no(last))
            def _():
                for copy in next_other:
                    copy.start()

    z_arrived(no(jnp.logical_or(outlet, beside)))
    turn(0)
    columns(1, 2)
    arrived(4)
    pass_on(both(inlet, no(zero)), 2)
    arrived(5)
    z_arrived(beside)
    turn(1)
    arrived(6, 7)
    pass_on(both(inlet, zero), 3)
    pass_on(both(origin, y == 0), 2)
    columns(3, 4)
    arrived(8, 9)
    pass_on(both(origin, y > 0), 2)
    near = sorted([(5, part) for part in FAR[0]] + [(6, part) for part in FAR[1]])
    far = sorted([(5, part) for part in FAR[1]] + [(6, part) for part in FAR[0]])

    @pl.when(jnp.logical_not(inlet))
    def _():
        image_arrived(2)
        image_arrived(3)

    turn(2)
    turn(3)
    arrived(10)
    columns(5, 6)
    scores(near)
    contribution(near)
    reduce_step(0, 1)
    scores(whole(0, 1, 2, 3, 4))
    arrived(11)
    scores(far)
    arrived(12)
    columns(7)
    opposite = sorted((7, part) for d in range(2) for part in FAR[d][:STEP])
    scores(opposite)
    contribution(opposite)
    reduce_step(2)
    arrived(13)
    opposite = sorted((7, part) for d in range(2) for part in FAR[d][STEP:])
    scores(opposite)
    contribution(opposite)
    reduce_step(3)
    g1[...] = image_term(1)

    @pl.when(jnp.logical_not(inlet))
    def _():
        for j in (2, 3, 0, 1):
            gis[half(j), :] = g1[half(j), :].astype(BF16)
            back[j].start()

    @pl.when(jnp.logical_not(has_next))
    def _():
        gir[0 : 2 * ROWS, :] = jnp.zeros((2 * ROWS, gir.shape[1]), BF16)

    contribution(whole(3, 4))
    reduce_step(4)
    contribution(far)
    reduce_step(5, 6)
    contribution(whole(1, 2))
    inlet_back(no(zero), 0)
    g0[...] = image_term(0)
    contribution(whole(0))
    inlet_back(no(zero), 1)
    reduce_step(7, 8)
    inlet_back(no(zero), 2)
    inlet_back(no(zero), 3)
    own_back(no(last), 0, 1)
    reduce_step(9)
    inlet_back(zero, 0)
    reduce_step(10)
    inlet_back(zero, 1)
    reduce_step(11)
    inlet_back(zero, 2)
    own_back(last, 0)
    reduce_step(12, 13)
    inlet_back(zero, 3)
    own_back(last, 1)

    @pl.when(has_next)
    def _():
        back_wait(0)
        back_wait(1)

    for copy in z_own:
        copy.wait_recv()
    gi_out[0] = (scale * (g0[:ROWS, :] + gir[:ROWS, :].astype(F32) + zr[...].astype(F32))).astype(BF16)
    for part in sorted(range(PARTS), key=lambda part: r_orders[0].index((1, part)) + r_orders[1].index((1, part))):
        total = ct[part * CHUNK : (part + 1) * CHUNK, :]
        for d in range(2):
            m = r_orders[d].index((1, part))
            reduction[d][m].wait_recv()
            total = total + rrecv[d, m * CHUNK : (m + 1) * CHUNK, :].astype(F32)
        gt_out[0, part * CHUNK : (part + 1) * CHUNK, :] = (scale * total).astype(BF16)

    def all_sent(ref, sem):
        pltpu.make_async_copy(ref, ref, sem).wait()

    def images_sent(*sems):
        for sem in sems:
            all_sent(img.at[pl.ds(0, ROWS)], im_s.at[sem])
            all_sent(meta.at[0], me_s.at[sem])

    all_sent(rrecv, ag_s)
    all_sent(rrecv, rs_s)
    all_sent(col.at[pl.ds(0, 7)], co_s)
    all_sent(gis, gi_s)
    all_sent(zs, zz_s)
    images_sent(0)

    @pl.when(has_next)
    def _():
        images_sent(1, 2)

    @pl.when(inlet)
    def _():
        images_sent(3, 4)


def write(gi, gt, gi_out, gt_out, sems):
    copies = [pltpu.make_async_copy(src, dst, sems.at[i]) for i, (src, dst) in enumerate(((gi, gi_out), (gt, gt_out)))]
    for copy in copies:
        copy.start()
    for copy in copies:
        copy.wait()


def body(image, text, logit_scale, lse_row, lse_col, pair):
    width = image.shape[2]
    msgs = 3 * PARTS + PARTS // 2
    hbm = pl.BlockSpec(memory_space=pltpu.HBM)
    dma = pltpu.SemaphoreType.DMA
    vmem = pl.BlockSpec(memory_space=pltpu.VMEM)
    out = pltpu.VMEM((1, ROWS, width), BF16)
    grads = pl.pallas_call(
        kernel,
        out_shape=(out, out),
        in_specs=[hbm, hbm, pl.BlockSpec(memory_space=pltpu.SMEM), hbm, hbm, hbm],
        out_specs=(vmem, vmem),
        scratch_shapes=[
            pltpu.VMEM((PLACES * ROWS, width), BF16),
            pltpu.VMEM((4 * ROWS, width), BF16),
            pltpu.VMEM((width, 4 * ROWS), BF16),
            pltpu.VMEM((4, 8, ROWS), F32),
            pltpu.VMEM((PLACES, 8, ROWS), F32),
            pltpu.VMEM((PLACES * ROWS, ROWS), F32),
            pltpu.VMEM((PLACES * ROWS, 4 * ROWS), BF16),
            pltpu.VMEM((PLACES * ROWS, width), F32),
            pltpu.VMEM((2, msgs * CHUNK, width), BF16),
            pltpu.VMEM((2, msgs * CHUNK, width), BF16),
            pltpu.VMEM((2 * ROWS, width), F32),
            pltpu.VMEM((2 * ROWS, width), F32),
            pltpu.VMEM((2 * ROWS, width), BF16),
            pltpu.VMEM((4 * ROWS, width), BF16),
            pltpu.VMEM((ROWS, width), BF16),
            pltpu.VMEM((ROWS, width), BF16),
            pltpu.VMEM((2, 1, ROWS), BF16),
            pltpu.VMEM((1, ROWS), jnp.int32),
            pltpu.SemaphoreType.REGULAR((4,)),
            dma((5,)),
            dma,
            dma,
            dma((2, msgs)),
            dma((5,)),
            dma((6,)),
            dma((5,)),
            dma((3,)),
            dma,
            dma((2, 4)),
            dma,
            dma((8,)),
            dma,
            dma((2,)),
        ],
        compiler_params=pltpu.CompilerParams(
            collective_id=0, has_side_effects=True, vmem_limit_bytes=63 * 2**20
        ),
        cost_estimate=pl.CostEstimate(
            flops=12 * ROWS * 16 * ROWS * width, bytes_accessed=8 * ROWS * width, transcendentals=8 * ROWS * 16 * ROWS
        ),
    )(image, text, jnp.reshape(logit_scale, (1,)), lse_row, lse_col, pair)
    return pl.pallas_call(
        write,
        out_shape=[jax.ShapeDtypeStruct((1, ROWS, width), BF16)] * 2,
        in_specs=[vmem, vmem],
        out_specs=[hbm, hbm],
        scratch_shapes=[dma((2,))],
        compiler_params=pltpu.CompilerParams(vmem_limit_bytes=2**20),
    )(*grads)


def solution(mesh):
    return jax.shard_map(
        body,
        mesh=mesh,
        in_specs=(
            P("blk", "grp", None),
            P("blk", "grp", None),
            P(),
            P("blk", "grp"),
            P("blk", "grp"),
            P("blk", "grp"),
        ),
        out_specs=(P("blk", "grp", None), P("blk", "grp", None)),
        check_vma=False,
    )
```

```python
import functools

import jax
import jax.numpy as jnp
from jax import lax
from jax.experimental import pallas as pl
from jax.experimental.pallas import tpu as pltpu
from jax.sharding import PartitionSpec as P

MESH = pl.DeviceIdType.MESH
RING = 8
ROWS = 128
PARTS = 4
STEP = PARTS // 4
CHUNK = ROWS // PARTS
HALF = ROWS // 2
PLACES = 8
RUN = 8
FAR = ((2, 3), (1, 0))
F32 = jnp.float32
BF16 = jnp.bfloat16


def place(direction, hops):
    return 0 if hops == 0 else 7 if hops == 4 else 2 * hops - 1 + direction


def gather_order(direction):
    far, near = FAR[direction], FAR[1 - direction]
    order = [(hop, part) for hop in (1, 2, 3) for part in far + near]
    return order + [(4, part) for part in far]


def reduce_order(direction):
    f0, f1 = FAR[direction][:STEP], FAR[direction][STEP:]
    n0, n1 = FAR[1 - direction][:STEP], FAR[1 - direction][STEP:]
    order = [
        (3, n0), (3, n1), (4, f0), (4, f1), (2, n0), (3, f0), (3, f1),
        (2, n1), (2, f0), (2, f1), (1, n0), (1, n1), (1, f0), (1, f1),
    ]
    return [(hops, part) for hops, parts in order for part in parts]


def kernel(
    image, text, scale_ref, lrow_ref, lcol_ref, pair_ref, gi_out, gt_out,
    txt, img, imgt, meta, col, lct, dt, ct, rsend, rrecv, g0, g1, gis, gir, zs, zr, vecs, pairs,
    ready, local_sem, ag_s, rs_s, ring_r, im_s, im_r, me_s, me_r, co_s, co_r, gi_s, gi_r, zz_s, zz_r,
):
    g = lax.axis_index("grp")
    b = lax.axis_index("blk")
    n_blk = lax.axis_size("blk")
    n_grp = 2 * RING
    zpart = g + 1 - 2 * lax.rem(g, 2)
    nxt = lax.rem(b + 1, n_blk)
    prv = lax.rem(b + n_blk - 1, n_blk)
    ring = [lax.rem(g + 2 * i, n_grp) for i in range(RING)]
    side = [ring[1], ring[7]]
    z_lo = lax.rem(g, 2)
    last = lax.rem(b, RUN) == RUN - 1
    first = lax.rem(b, RUN) == 0
    zero = b == 0
    low, high = z_lo == 0, z_lo == 1
    no = jnp.logical_not
    both = jnp.logical_and
    has_next = no(both(last, low))
    has_prev = no(both(first, high))
    outlet = both(last, high)
    inlet = both(first, low)
    next_grp = jnp.where(last, zpart, g)
    prev_grp = jnp.where(first, zpart, g)

    y = g // 2
    origin = both(zero, low)
    left_first = jnp.where(y == 0, origin, both(y < 7, no(both(origin, y == 1))))
    right_first = jnp.where(y == 0, origin, jnp.where(y == 7, no(origin), y == 6))
    z_first = jnp.where(jnp.logical_or(both(zero, y == 0), nxt == 0), low, high)
    prev_first = both(has_prev, no(jnp.logical_or(zero, both(b == 1, both(y == 0, low)))))
    next_first = both(has_next, jnp.logical_or(nxt == 0, both(origin, y == 0)))
    direct_from = both(both(zero, y == 0), high)
    direct_to = both(both(nxt == 0, y == 0), outlet)
    meets = (
        (left_first, True, side[1], b, 1),
        (right_first, True, side[0], b, 0),
        (z_first, True, zpart, b, 2),
        (prev_first, has_prev, prev_grp, prv, 3),
        (next_first, has_next, next_grp, nxt, None),
        (direct_to, both(direct_from, True), g, prv, None),
    )
    barrier = pltpu.get_barrier_semaphore()

    def greet(grp, blk, sem):
        pl.semaphore_signal(sem, inc=1, device_id={"grp": grp, "blk": blk}, device_id_type=MESH)

    for they_first, met, grp, blk, _ in meets:

        @pl.when(both(met, no(they_first)))
        def _(grp=grp, blk=blk):
            greet(grp, blk, barrier)

    def copy_to(src, dst, s_sem, r_sem, grp=g, blk=b):
        return pltpu.make_async_remote_copy(
            src_ref=src, dst_ref=dst, send_sem=s_sem, recv_sem=r_sem,
            device_id={"grp": grp, "blk": blk}, device_id_type=MESH,
        )

    local = [
        pltpu.make_async_copy(src, dst, local_sem.at[i])
        for i, (src, dst) in enumerate((
            (pair_ref, pairs),
            (lrow_ref, vecs.at[0]),
            (lcol_ref, vecs.at[1]),
            (text.at[0], txt.at[pl.ds(0, ROWS)]),
            (image.at[0], img.at[pl.ds(0, ROWS)]),
        ))
    ]
    for copy in local:
        copy.start()
    scale = scale_ref[0]

    def go(copy):
        copy.start()

    orders = [gather_order(0), gather_order(1)]

    def gather_copy(direction, n):
        hop, part = orders[direction][n]
        rows = lambda p: txt.at[pl.ds(p * ROWS + part * CHUNK, CHUNK)]
        src = text.at[0, pl.ds(part * CHUNK, CHUNK)] if hop == 1 else rows(place(direction, hop - 1))
        return copy_to(
            src, rows(place(direction, hop)), ag_s, ring_r.at[direction, n], grp=side[direction]
        )

    def col_copy(direction, hop):
        return copy_to(
            col.at[place(direction, hop - 1)], col.at[place(direction, hop)],
            co_s, co_r.at[direction, hop - 1], grp=side[direction],
        )

    gather = [[gather_copy(d, n) for n in range(len(orders[d]))] for d in range(2)]
    cols = [[col_copy(0, hop) for hop in (1, 2, 3, 4)], [col_copy(1, hop) for hop in (1, 2, 3)]]

    def arrived(*steps):
        for n in [STEP * step + i for step in steps for i in range(STEP)]:
            hop = n // PARTS + 1
            for d in range(2):
                if n % PARTS == 0 and hop <= len(cols[d]):
                    cols[d][hop - 1].wait_recv()
                    if hop < len(cols[d]):
                        go(cols[d][hop])
                gather[d][n].wait_recv()
                if n + PARTS < len(orders[d]):
                    go(gather[d][n + PARTS])

    def image_copies(src, dst, sem, **to):
        def copy(i):
            start = i * HALF
            rows = image.at[0, pl.ds(start, HALF)] if src == 0 else img.at[pl.ds(src * ROWS + start, HALF)]
            r_sem = im_r.at[2 * (dst - 1) + i]
            return copy_to(rows, img.at[pl.ds(dst * ROWS + start, HALF)], im_s.at[sem], r_sem, **to)

        return copy(0), copy(1), copy_to(meta.at[src], meta.at[dst], me_s.at[sem], me_r.at[dst - 1], **to)

    swap = last.astype(jnp.int32)
    z_img = image_copies(0, 1, 0, grp=zpart)
    next_own = image_copies(0, 2 + swap, 1, grp=next_grp, blk=nxt)
    next_other = image_copies(1, 3 - swap, 2, grp=next_grp, blk=nxt)
    passed = {3: image_copies(3, 2, 3, grp=zpart), 2: image_copies(2, 3, 4, grp=zpart)}
    direct = image_copies(1, 3, 5, grp=g, blk=nxt)
    arrivals = {2: image_copies(0, 2, 0, grp=zpart), 3: image_copies(0, 3, 0, grp=zpart)}

    def image_arrived(slot):
        for copy in arrivals[slot]:
            copy.wait_recv()

    def start_if(condition, copies):
        @pl.when(condition)
        def _():
            for copy in copies:
                copy.start()

    def pass_on(condition, slot, skip=False):
        @pl.when(condition)
        def _():
            for got, copy in zip(arrivals[slot], passed[slot]):
                got.wait_recv()
                if not skip:
                    copy.start()

    def take(ref, parts):
        pieces = []
        for p, part in parts:
            lo = p * ROWS + part * CHUNK
            if pieces and pieces[-1][1] == lo:
                pieces[-1][1] = lo + CHUNK
            else:
                pieces.append([lo, lo + CHUNK])
        pieces = [ref[lo:hi, :] for lo, hi in pieces]
        return pieces[0] if len(pieces) == 1 else jnp.concatenate(pieces, axis=0)

    def whole(*places):
        return [(p, part) for p in places for part in range(PARTS)]

    def columns(*places):
        for p in places:
            lct[p * ROWS : (p + 1) * ROWS, :] = jnp.broadcast_to(col[p, 0:1, :], (ROWS, ROWS)).T

    def turn(slot):
        imgt[:, slot * ROWS : (slot + 1) * ROWS] = img[slot * ROWS : (slot + 1) * ROWS, :].T

    def scores(parts):
        s = jnp.dot(take(txt, parts), imgt[...], preferred_element_type=F32) * scale
        lr = jnp.concatenate([meta[slot, 0:1, :] for slot in range(4)], axis=1)
        lc = take(lct, parts)
        d = 0.5 * (jnp.exp(s - lr) + jnp.exp(s - jnp.concatenate([lc] * 4, axis=1)))
        pr = jnp.concatenate([meta[0, 1:2, :], meta[1, 1:2, :]], axis=1).astype(jnp.int32)
        iota = lax.broadcasted_iota(jnp.int32, (CHUNK, 2 * ROWS), 0)
        for i, (p, part) in enumerate(parts):
            rel = 0 if p == 0 else 4 if p == 7 else (RING - (p + 1) // 2) if p % 2 else p // 2
            rows = d[i * CHUNK : (i + 1) * CHUNK]
            own = rows[:, : 2 * ROWS] - (pr - (ring[rel] * ROWS + part * CHUNK) == iota).astype(F32)
            lo = p * ROWS + part * CHUNK
            dt[lo : lo + CHUNK, : 2 * ROWS] = own.astype(BF16)
            dt[lo : lo + CHUNK, 2 * ROWS :] = rows[:, 2 * ROWS :].astype(BF16)

    def contribution(parts):
        c = jnp.dot(take(dt, parts), img[...], preferred_element_type=F32)
        for i, (p, part) in enumerate(parts):
            lo = p * ROWS + part * CHUNK
            ct[lo : lo + CHUNK, :] = c[i * CHUNK : (i + 1) * CHUNK]

    def image_term(k):
        return lax.dot_general(
            dt[:, k * 2 * ROWS : (k + 1) * 2 * ROWS], txt[...], (((0,), (0,)), ((), ())), preferred_element_type=F32
        )

    r_orders = [reduce_order(0), reduce_order(1)]

    def reduce_copy(direction, n):
        rows = pl.ds(n * CHUNK, CHUNK)
        return copy_to(
            rsend.at[direction, rows], rrecv.at[direction, rows],
            rs_s, ring_r.at[direction, n], grp=side[direction],
        )

    reduction = [[reduce_copy(d, n) for n in range(len(r_orders[d]))] for d in range(2)]

    def reduce_step(*steps):
        for n in [STEP * step + i for step in steps for i in range(STEP)]:
            for d in range(2):
                hops, part = r_orders[d][n]
                start = place(1 - d, hops) * ROWS + part * CHUNK
                total = ct[start : start + CHUNK, :]
                if (hops + 1, part) in r_orders[d]:
                    m = r_orders[d].index((hops + 1, part))
                    reduction[d][m].wait_recv()
                    total = total + rrecv[d, m * CHUNK : (m + 1) * CHUNK, :].astype(F32)
                rsend[d, n * CHUNK : (n + 1) * CHUNK, :] = total.astype(BF16)
                go(reduction[d][n])

    half = lambda j: slice(j * HALF, (j + 1) * HALF)
    feeder = jnp.logical_and(first, z_lo == 1)
    back_blk = jnp.where(feeder, b, prv)

    def back_copy(j):
        if j < 2:
            to = jnp.where(feeder, j + 6, jnp.where(inlet, j + 2, j))
        else:
            to = jnp.where(feeder, j + 2, jnp.where(inlet, j - 2, j))
        return copy_to(
            gis.at[pl.ds(j * HALF, HALF)], gir.at[pl.ds(pl.multiple_of(to * HALF, HALF), HALF)],
            gi_s, gi_r.at[to], grp=prev_grp, blk=back_blk,
        )

    back = [back_copy(j) for j in range(4)]

    def back_wait(to):
        rows = pl.ds(to * HALF, HALF)
        copy_to(gis.at[pl.ds(0, HALF)], gir.at[rows], gi_s, gi_r.at[to], grp=zpart).wait_recv()

    def inlet_back(condition, j):
        @pl.when(both(inlet, condition))
        def _():
            back_wait(4 + j)
            gis[half(j), :] = (g1[half(j), :] + gir[half(4 + j), :].astype(F32)).astype(BF16)
            back[j].start()

    z_own = [
        copy_to(zs.at[pl.ds(i * HALF, HALF)], zr.at[pl.ds(i * HALF, HALF)], zz_s, zz_r.at[i], grp=zpart)
        for i in range(2)
    ]

    def own_back(condition, *halves):
        @pl.when(condition)
        def _():
            for i in halves:

                @pl.when(has_next)
                def _():
                    back_wait(2 + i)

                zs[half(i), :] = (g0[half(2 + i), :] + gir[half(2 + i), :].astype(F32)).astype(BF16)
                z_own[i].start()

    behind = jnp.logical_or(y < 2, y == RING - 1)

    greeted = sum(they_first.astype(jnp.int32) for they_first, *_ in meets)

    @pl.when(greeted > 0)
    def _():
        pl.semaphore_wait(barrier, greeted)

    for they_first, _, grp, blk, sem in meets:
        if sem is not None:

            @pl.when(they_first)
            def _(grp=grp, blk=blk, sem=sem):
                greet(grp, blk, ready.at[sem])

    for copy in local[:3]:
        copy.wait()
    meta[0] = jnp.zeros((8, ROWS), F32)
    meta[0, 0:1, :] = vecs[0].astype(F32)
    meta[0, 1:2, :] = pairs[...].astype(F32)
    col[0] = jnp.broadcast_to(vecs[1].astype(F32), (8, ROWS))

    def open_side(condition, d, answer):
        @pl.when(condition)
        def _():
            if answer:
                pl.semaphore_wait(ready.at[1 - d], 1)
            cols[d][0].start()
            for n in range(PARTS):
                gather[d][n].start()

    open_side(left_first, 1, False)
    open_side(right_first, 0, False)
    beside = lax.rem(b, RUN) == RUN - 2
    held = jnp.logical_or(beside, both(both(zero, y == 0), high))

    def open_z(condition):
        @pl.when(condition)
        def _():
            @pl.when(no(z_first))
            def _():
                pl.semaphore_wait(ready.at[2], 1)

            for copy in z_img:
                copy.start()

    open_z(last)
    open_side(no(right_first), 0, True)
    open_side(no(left_first), 1, True)
    open_z(no(jnp.logical_or(held, last)))

    @pl.when(has_next)
    def _():
        @pl.when(no(next_first))
        def _():
            pl.semaphore_wait(ready.at[3], 1)

        for copy in next_own:
            copy.start()

    for copy in local[3:]:
        copy.wait()
    columns(0)
    arrived(0)

    @pl.when(outlet)
    def _():
        z_img[0].wait_recv()
        next_other[0].start()
        pl.when(direct_to)(direct[0].start)

    arrived(1)
    open_z(held)

    @pl.when(outlet)
    def _():
        for got, copy, more in zip(z_img[1:], next_other[1:], direct[1:]):
            got.wait_recv()
            copy.start()
            pl.when(direct_to)(more.start)

    arrived(2)
    pass_on(both(inlet, no(zero)), 3)
    arrived(3)

    def z_arrived(condition):
        @pl.when(condition)
        def _():
            for copy in z_img:
                copy.wait_recv()

            @pl.when(no(last))
            def _():
                for copy in next_other:
                    copy.start()

    z_arrived(no(jnp.logical_or(outlet, beside)))
    turn(0)
    columns(1, 2)
    arrived(4)
    pass_on(both(inlet, no(zero)), 2)
    arrived(5)
    z_arrived(beside)
    turn(1)
    pass_on(both(origin, behind), 3)
    arrived(6, 7)
    pass_on(both(origin, no(behind)), 3)
    pass_on(both(origin, both(behind, y > 0)), 2)
    columns(3, 4)
    arrived(8)
    pass_on(both(origin, no(behind)), 2)
    arrived(9)
    pass_on(both(origin, y == 0), 2, skip=True)
    near = sorted([(5, part) for part in FAR[0]] + [(6, part) for part in FAR[1]])
    far = sorted([(5, part) for part in FAR[1]] + [(6, part) for part in FAR[0]])

    @pl.when(jnp.logical_not(inlet))
    def _():
        image_arrived(2)
        image_arrived(3)

    turn(2)
    turn(3)
    arrived(10)
    columns(5, 6)
    scores(near)
    contribution(near)
    reduce_step(0, 1)
    scores(whole(0, 1, 2, 3, 4))
    arrived(11)
    scores(far)
    arrived(12)
    columns(7)
    opposite = sorted((7, part) for d in range(2) for part in FAR[d][:STEP])
    scores(opposite)
    contribution(opposite)
    reduce_step(2)
    contribution(whole(3, 4))
    contribution(far)
    arrived(13)
    opposite = sorted((7, part) for d in range(2) for part in FAR[d][STEP:])
    scores(opposite)
    contribution(opposite)
    reduce_step(3, 4)
    g1[...] = image_term(1)

    @pl.when(jnp.logical_not(inlet))
    def _():
        for j in (2, 3, 0, 1):
            gis[half(j), :] = g1[half(j), :].astype(BF16)
            back[j].start()

    @pl.when(jnp.logical_not(has_next))
    def _():
        gir[0 : 2 * ROWS, :] = jnp.zeros((2 * ROWS, gir.shape[1]), BF16)

    contribution(whole(1, 2))
    g0[...] = image_term(0)
    contribution(whole(0))
    reduce_step(5, 6, 7)
    inlet_back(no(zero), 0)
    inlet_back(no(zero), 1)
    reduce_step(8)
    own_back(no(last), 0, 1)
    reduce_step(9)
    inlet_back(no(zero), 2)
    reduce_step(10)
    inlet_back(no(zero), 3)
    reduce_step(11)
    own_back(last, 0)
    inlet_back(zero, 0)
    inlet_back(zero, 1)
    reduce_step(12, 13)
    inlet_back(zero, 2)
    inlet_back(zero, 3)
    own_back(last, 1)

    @pl.when(has_next)
    def _():
        back_wait(0)
        back_wait(1)

    for copy in z_own:
        copy.wait_recv()
    gi_out[0] = (scale * (g0[:ROWS, :] + gir[:ROWS, :].astype(F32) + zr[...].astype(F32))).astype(BF16)
    for part in sorted(range(PARTS), key=lambda part: r_orders[0].index((1, part)) + r_orders[1].index((1, part))):
        total = ct[part * CHUNK : (part + 1) * CHUNK, :]
        for d in range(2):
            m = r_orders[d].index((1, part))
            reduction[d][m].wait_recv()
            total = total + rrecv[d, m * CHUNK : (m + 1) * CHUNK, :].astype(F32)
        gt_out[0, part * CHUNK : (part + 1) * CHUNK, :] = (scale * total).astype(BF16)

    def all_sent(ref, sem):
        pltpu.make_async_copy(ref, ref, sem).wait()

    def images_sent(*sems):
        for sem in sems:
            all_sent(img.at[pl.ds(0, ROWS)], im_s.at[sem])
            all_sent(meta.at[0], me_s.at[sem])

    all_sent(rrecv, ag_s)
    all_sent(rrecv, rs_s)
    all_sent(col.at[pl.ds(0, 7)], co_s)
    all_sent(gis, gi_s)
    all_sent(zs, zz_s)
    images_sent(0)

    @pl.when(has_next)
    def _():
        images_sent(1, 2)

    @pl.when(inlet)
    def _():
        images_sent(3)

    @pl.when(both(inlet, no(both(origin, y == 0))))
    def _():
        images_sent(4)

    @pl.when(direct_to)
    def _():
        images_sent(5)


def write(gi, gt, gi_out, gt_out, sems):
    copies = [
        pltpu.make_async_copy(src, dst, sems.at[i])
        for i, (src, dst) in enumerate(((gi, gi_out), (gt, gt_out)))
    ]
    for copy in copies:
        copy.start()
    for copy in copies:
        copy.wait()


def body(image, text, logit_scale, lse_row, lse_col, pair):
    width = image.shape[2]
    msgs = 3 * PARTS + PARTS // 2
    hbm = pl.BlockSpec(memory_space=pltpu.HBM)
    dma = pltpu.SemaphoreType.DMA
    vmem = pl.BlockSpec(memory_space=pltpu.VMEM)
    out = pltpu.VMEM((1, ROWS, width), BF16)
    grads = pl.pallas_call(
        kernel,
        out_shape=(out, out),
        in_specs=[hbm, hbm, pl.BlockSpec(memory_space=pltpu.SMEM), hbm, hbm, hbm],
        out_specs=(vmem, vmem),
        scratch_shapes=[
            pltpu.VMEM((PLACES * ROWS, width), BF16),
            pltpu.VMEM((4 * ROWS, width), BF16),
            pltpu.VMEM((width, 4 * ROWS), BF16),
            pltpu.VMEM((4, 8, ROWS), F32),
            pltpu.VMEM((PLACES, 8, ROWS), F32),
            pltpu.VMEM((PLACES * ROWS, ROWS), F32),
            pltpu.VMEM((PLACES * ROWS, 4 * ROWS), BF16),
            pltpu.VMEM((PLACES * ROWS, width), F32),
            pltpu.VMEM((2, msgs * CHUNK, width), BF16),
            pltpu.VMEM((2, msgs * CHUNK, width), BF16),
            pltpu.VMEM((2 * ROWS, width), F32),
            pltpu.VMEM((2 * ROWS, width), F32),
            pltpu.VMEM((2 * ROWS, width), BF16),
            pltpu.VMEM((4 * ROWS, width), BF16),
            pltpu.VMEM((ROWS, width), BF16),
            pltpu.VMEM((ROWS, width), BF16),
            pltpu.VMEM((2, 1, ROWS), BF16),
            pltpu.VMEM((1, ROWS), jnp.int32),
            pltpu.SemaphoreType.REGULAR((4,)),
            dma((5,)),
            dma,
            dma,
            dma((2, msgs)),
            dma((6,)),
            dma((6,)),
            dma((6,)),
            dma((3,)),
            dma,
            dma((2, 4)),
            dma,
            dma((8,)),
            dma,
            dma((2,)),
        ],
        compiler_params=pltpu.CompilerParams(
            collective_id=0, has_side_effects=True, vmem_limit_bytes=63 * 2**20
        ),
        cost_estimate=pl.CostEstimate(
            flops=12 * ROWS * 16 * ROWS * width, bytes_accessed=8 * ROWS * width, transcendentals=8 * ROWS * 16 * ROWS
        ),
    )(image, text, jnp.reshape(logit_scale, (1,)), lse_row, lse_col, pair)
    return pl.pallas_call(
        write,
        out_shape=[jax.ShapeDtypeStruct((1, ROWS, width), BF16)] * 2,
        in_specs=[vmem, vmem],
        out_specs=[hbm, hbm],
        scratch_shapes=[dma((2,))],
        compiler_params=pltpu.CompilerParams(vmem_limit_bytes=2**20),
    )(*grads)


def solution(mesh):
    return jax.shard_map(
        body,
        mesh=mesh,
        in_specs=(
            P("blk", "grp", None),
            P("blk", "grp", None),
            P(),
            P("blk", "grp"),
            P("blk", "grp"),
            P("blk", "grp"),
        ),
        out_specs=(P("blk", "grp", None), P("blk", "grp", None)),
        check_vma=False,
    )
```

```python
import functools

import jax
import jax.numpy as jnp
from jax import lax
from jax.experimental import pallas as pl
from jax.experimental.pallas import tpu as pltpu
from jax.sharding import PartitionSpec as P

MESH = pl.DeviceIdType.MESH
RING = 8
ROWS = 128
PARTS = 4
STEP = PARTS // 4
CHUNK = ROWS // PARTS
HALF = ROWS // 2
PLACES = 8
RUN = 8
FAR = ((2, 3), (1, 0))
F32 = jnp.float32
BF16 = jnp.bfloat16


def place(direction, hops):
    return 0 if hops == 0 else 7 if hops == 4 else 2 * hops - 1 + direction


def gather_order(direction):
    far, near = FAR[direction], FAR[1 - direction]
    order = [(hop, part) for hop in (1, 2, 3) for part in far + near]
    return order + [(4, part) for part in far]


def reduce_order(direction):
    f0, f1 = FAR[direction][:STEP], FAR[direction][STEP:]
    n0, n1 = FAR[1 - direction][:STEP], FAR[1 - direction][STEP:]
    order = [
        (3, n0), (3, n1), (4, f0), (4, f1), (2, n0), (3, f0), (3, f1),
        (2, n1), (2, f0), (2, f1), (1, n0), (1, n1), (1, f0), (1, f1),
    ]
    return [(hops, part) for hops, parts in order for part in parts]


def kernel(
    image, text, scale_ref, lrow_ref, lcol_ref, pair_ref, gi_out, gt_out,
    txt, img, imgt, meta, col, lct, dt, ct, rsend, rrecv, g0, g1, gis, gir, zs, zr, vecs, pairs,
    ready, local_sem, ag_s, rs_s, ring_r, im_s, im_r, me_s, me_r, co_s, co_r, gi_s, gi_r, zz_s, zz_r,
):
    g = lax.axis_index("grp")
    b = lax.axis_index("blk")
    n_blk = lax.axis_size("blk")
    n_grp = 2 * RING
    zpart = g + 1 - 2 * lax.rem(g, 2)
    nxt = lax.rem(b + 1, n_blk)
    prv = lax.rem(b + n_blk - 1, n_blk)
    ring = [lax.rem(g + 2 * i, n_grp) for i in range(RING)]
    side = [ring[1], ring[7]]
    z_lo = lax.rem(g, 2)
    last = lax.rem(b, RUN) == RUN - 1
    first = lax.rem(b, RUN) == 0
    zero = b == 0
    low, high = z_lo == 0, z_lo == 1
    no = jnp.logical_not
    both = jnp.logical_and
    has_next = no(both(last, low))
    has_prev = no(both(first, high))
    outlet = both(last, high)
    inlet = both(first, low)
    next_grp = jnp.where(last, zpart, g)
    prev_grp = jnp.where(first, zpart, g)

    y = g // 2
    origin = both(zero, low)
    left_first = jnp.where(y == 0, origin, both(y < 7, no(both(origin, y == 1))))
    right_first = jnp.where(y == 0, origin, jnp.where(y == 7, no(origin), y == 6))
    z_first = jnp.where(jnp.logical_or(both(zero, y == 0), nxt == 0), low, high)
    early = lambda blk: jnp.logical_or(blk == 0, blk == n_blk - RUN)
    prev_first = both(has_prev, no(jnp.logical_or(early(b), both(b == 1, both(y == 0, low)))))
    next_first = both(has_next, jnp.logical_or(early(nxt), both(origin, y == 0)))
    direct_from = both(zero, high)
    direct_to = both(nxt == 0, low)
    meets = (
        (left_first, True, side[1], b, 1),
        (right_first, True, side[0], b, 0),
        (z_first, True, zpart, b, 2),
        (prev_first, has_prev, prev_grp, prv, 3),
        (next_first, has_next, next_grp, nxt, None),
        (direct_to, direct_from, zpart, prv, None),
    )
    barrier = pltpu.get_barrier_semaphore()

    def greet(grp, blk, sem):
        pl.semaphore_signal(sem, inc=1, device_id={"grp": grp, "blk": blk}, device_id_type=MESH)

    for they_first, met, grp, blk, _ in meets:

        @pl.when(both(met, no(they_first)))
        def _(grp=grp, blk=blk):
            greet(grp, blk, barrier)

    def copy_to(src, dst, s_sem, r_sem, grp=g, blk=b):
        return pltpu.make_async_remote_copy(
            src_ref=src, dst_ref=dst, send_sem=s_sem, recv_sem=r_sem,
            device_id={"grp": grp, "blk": blk}, device_id_type=MESH,
        )

    local = [
        pltpu.make_async_copy(src, dst, local_sem.at[i])
        for i, (src, dst) in enumerate((
            (pair_ref, pairs),
            (lrow_ref, vecs.at[0]),
            (lcol_ref, vecs.at[1]),
            (text.at[0], txt.at[pl.ds(0, ROWS)]),
            (image.at[0], img.at[pl.ds(0, ROWS)]),
        ))
    ]
    for copy in local:
        copy.start()
    scale = scale_ref[0]

    def go(copy):
        copy.start()

    orders = [gather_order(0), gather_order(1)]

    def gather_copy(direction, n):
        hop, part = orders[direction][n]
        rows = lambda p: txt.at[pl.ds(p * ROWS + part * CHUNK, CHUNK)]
        src = text.at[0, pl.ds(part * CHUNK, CHUNK)] if hop == 1 else rows(place(direction, hop - 1))
        return copy_to(
            src, rows(place(direction, hop)), ag_s, ring_r.at[direction, n], grp=side[direction]
        )

    def col_copy(direction, hop):
        return copy_to(
            col.at[place(direction, hop - 1)], col.at[place(direction, hop)],
            co_s, co_r.at[direction, hop - 1], grp=side[direction],
        )

    gather = [[gather_copy(d, n) for n in range(len(orders[d]))] for d in range(2)]
    cols = [[col_copy(0, hop) for hop in (1, 2, 3, 4)], [col_copy(1, hop) for hop in (1, 2, 3)]]

    def arrived(*steps):
        for n in [STEP * step + i for step in steps for i in range(STEP)]:
            hop = n // PARTS + 1
            for d in range(2):
                if n % PARTS == 0 and hop <= len(cols[d]):
                    cols[d][hop - 1].wait_recv()
                    if hop < len(cols[d]):
                        go(cols[d][hop])
                gather[d][n].wait_recv()
                if n + PARTS < len(orders[d]):
                    go(gather[d][n + PARTS])

    def image_copies(src, dst, sem, **to):
        def copy(i):
            start = i * HALF
            rows = image.at[0, pl.ds(start, HALF)] if src == 0 else img.at[pl.ds(src * ROWS + start, HALF)]
            r_sem = im_r.at[2 * (dst - 1) + i]
            return copy_to(rows, img.at[pl.ds(dst * ROWS + start, HALF)], im_s.at[sem], r_sem, **to)

        return copy(0), copy(1), copy_to(meta.at[src], meta.at[dst], me_s.at[sem], me_r.at[dst - 1], **to)

    swap = last.astype(jnp.int32)
    z_img = image_copies(0, 1, 0, grp=zpart)
    next_own = image_copies(0, 2 + swap, 1, grp=next_grp, blk=nxt)
    next_other = image_copies(1, 3 - swap, 2, grp=next_grp, blk=nxt)
    passed = {3: image_copies(3, 2, 3, grp=zpart), 2: image_copies(2, 3, 4, grp=zpart)}
    direct = image_copies(0, 3, 5, grp=zpart, blk=nxt)
    arrivals = {2: image_copies(0, 2, 0, grp=zpart), 3: image_copies(0, 3, 0, grp=zpart)}

    def image_arrived(slot):
        for copy in arrivals[slot]:
            copy.wait_recv()

    def start_if(condition, copies):
        @pl.when(condition)
        def _():
            for copy in copies:
                copy.start()

    def pass_on(condition, slot):
        @pl.when(condition)
        def _():
            for got, copy in zip(arrivals[slot], passed[slot]):
                got.wait_recv()
                copy.start()

    def take(ref, parts):
        pieces = []
        for p, part in parts:
            lo = p * ROWS + part * CHUNK
            if pieces and pieces[-1][1] == lo:
                pieces[-1][1] = lo + CHUNK
            else:
                pieces.append([lo, lo + CHUNK])
        pieces = [ref[lo:hi, :] for lo, hi in pieces]
        return pieces[0] if len(pieces) == 1 else jnp.concatenate(pieces, axis=0)

    def whole(*places):
        return [(p, part) for p in places for part in range(PARTS)]

    def columns(*places):
        for p in places:
            lct[p * ROWS : (p + 1) * ROWS, :] = jnp.broadcast_to(col[p, 0:1, :], (ROWS, ROWS)).T

    def turn(slot):
        imgt[:, slot * ROWS : (slot + 1) * ROWS] = img[slot * ROWS : (slot + 1) * ROWS, :].T

    def scores(parts):
        s = jnp.dot(take(txt, parts), imgt[...], preferred_element_type=F32) * scale
        lr = jnp.concatenate([meta[slot, 0:1, :] for slot in range(4)], axis=1)
        lc = take(lct, parts)
        d = 0.5 * (jnp.exp(s - lr) + jnp.exp(s - jnp.concatenate([lc] * 4, axis=1)))
        pr = jnp.concatenate([meta[0, 1:2, :], meta[1, 1:2, :]], axis=1).astype(jnp.int32)
        iota = lax.broadcasted_iota(jnp.int32, (CHUNK, 2 * ROWS), 0)
        for i, (p, part) in enumerate(parts):
            rel = 0 if p == 0 else 4 if p == 7 else (RING - (p + 1) // 2) if p % 2 else p // 2
            rows = d[i * CHUNK : (i + 1) * CHUNK]
            own = rows[:, : 2 * ROWS] - (pr - (ring[rel] * ROWS + part * CHUNK) == iota).astype(F32)
            lo = p * ROWS + part * CHUNK
            dt[lo : lo + CHUNK, : 2 * ROWS] = own.astype(BF16)
            dt[lo : lo + CHUNK, 2 * ROWS :] = rows[:, 2 * ROWS :].astype(BF16)

    def contribution(parts):
        c = jnp.dot(take(dt, parts), img[...], preferred_element_type=F32)
        for i, (p, part) in enumerate(parts):
            lo = p * ROWS + part * CHUNK
            ct[lo : lo + CHUNK, :] = c[i * CHUNK : (i + 1) * CHUNK]

    def image_term(k):
        return lax.dot_general(
            dt[:, k * 2 * ROWS : (k + 1) * 2 * ROWS], txt[...], (((0,), (0,)), ((), ())), preferred_element_type=F32
        )

    r_orders = [reduce_order(0), reduce_order(1)]

    def reduce_copy(direction, n):
        rows = pl.ds(n * CHUNK, CHUNK)
        return copy_to(
            rsend.at[direction, rows], rrecv.at[direction, rows],
            rs_s, ring_r.at[direction, n], grp=side[direction],
        )

    reduction = [[reduce_copy(d, n) for n in range(len(r_orders[d]))] for d in range(2)]

    def reduce_step(*steps):
        for n in [STEP * step + i for step in steps for i in range(STEP)]:
            for d in range(2):
                hops, part = r_orders[d][n]
                start = place(1 - d, hops) * ROWS + part * CHUNK
                total = ct[start : start + CHUNK, :]
                if (hops + 1, part) in r_orders[d]:
                    m = r_orders[d].index((hops + 1, part))
                    reduction[d][m].wait_recv()
                    total = total + rrecv[d, m * CHUNK : (m + 1) * CHUNK, :].astype(F32)
                rsend[d, n * CHUNK : (n + 1) * CHUNK, :] = total.astype(BF16)
                go(reduction[d][n])

    half = lambda j: slice(j * HALF, (j + 1) * HALF)
    feeder = jnp.logical_and(first, z_lo == 1)
    back_blk = jnp.where(feeder, b, prv)

    def back_copy(j):
        if j < 2:
            to = jnp.where(feeder, j + 6, jnp.where(inlet, j + 2, j))
        else:
            to = jnp.where(feeder, j + 2, jnp.where(inlet, j - 2, j))
        return copy_to(
            gis.at[pl.ds(j * HALF, HALF)], gir.at[pl.ds(pl.multiple_of(to * HALF, HALF), HALF)],
            gi_s, gi_r.at[to], grp=prev_grp, blk=back_blk,
        )

    back = [back_copy(j) for j in range(4)]

    def back_wait(to):
        rows = pl.ds(to * HALF, HALF)
        copy_to(gis.at[pl.ds(0, HALF)], gir.at[rows], gi_s, gi_r.at[to], grp=zpart).wait_recv()

    def inlet_back(condition, j):
        @pl.when(both(inlet, condition))
        def _():
            back_wait(4 + j)
            gis[half(j), :] = (g1[half(j), :] + gir[half(4 + j), :].astype(F32)).astype(BF16)
            back[j].start()

    z_own = [
        copy_to(zs.at[pl.ds(i * HALF, HALF)], zr.at[pl.ds(i * HALF, HALF)], zz_s, zz_r.at[i], grp=zpart)
        for i in range(2)
    ]

    def own_back(condition, *halves):
        @pl.when(condition)
        def _():
            for i in halves:

                @pl.when(has_next)
                def _():
                    back_wait(2 + i)

                zs[half(i), :] = (g0[half(2 + i), :] + gir[half(2 + i), :].astype(F32)).astype(BF16)
                z_own[i].start()

    behind = jnp.logical_or(y < 2, y == RING - 1)

    greeted = sum(they_first.astype(jnp.int32) for they_first, *_ in meets)

    @pl.when(greeted > 0)
    def _():
        pl.semaphore_wait(barrier, greeted)

    for they_first, _, grp, blk, sem in meets:
        if sem is not None:

            @pl.when(they_first)
            def _(grp=grp, blk=blk, sem=sem):
                greet(grp, blk, ready.at[sem])

    for copy in local[:3]:
        copy.wait()
    meta[0] = jnp.zeros((8, ROWS), F32)
    meta[0, 0:1, :] = vecs[0].astype(F32)
    meta[0, 1:2, :] = pairs[...].astype(F32)
    col[0] = jnp.broadcast_to(vecs[1].astype(F32), (8, ROWS))

    def open_side(condition, d, answer):
        @pl.when(condition)
        def _():
            if answer:
                pl.semaphore_wait(ready.at[1 - d], 1)
            cols[d][0].start()
            for n in range(PARTS):
                gather[d][n].start()

    open_side(left_first, 1, False)
    open_side(right_first, 0, False)
    beside = lax.rem(b, RUN) == RUN - 2
    held = jnp.logical_or(beside, both(both(zero, y == 0), high))

    def open_z(condition):
        @pl.when(condition)
        def _():
            @pl.when(no(z_first))
            def _():
                pl.semaphore_wait(ready.at[2], 1)

            for copy in z_img:
                copy.start()

    open_z(last)

    def open_next(condition):
        @pl.when(both(has_next, condition))
        def _():
            @pl.when(no(next_first))
            def _():
                pl.semaphore_wait(ready.at[3], 1)

            for copy in next_own:
                copy.start()

    open_next(next_first)
    open_side(no(right_first), 0, True)
    open_side(no(left_first), 1, True)
    open_z(no(jnp.logical_or(held, last)))

    open_next(no(next_first))
    for copy in local[3:]:
        copy.wait()
    columns(0)
    arrived(0)
    start_if(direct_to, direct)

    @pl.when(outlet)
    def _():
        z_img[0].wait_recv()
        next_other[0].start()

    arrived(1)
    open_z(held)

    @pl.when(outlet)
    def _():
        for got, copy in zip(z_img[1:], next_other[1:]):
            got.wait_recv()
            copy.start()

    arrived(2)
    pass_on(both(inlet, no(zero)), 3)
    arrived(3)

    def z_arrived(condition):
        @pl.when(condition)
        def _():
            for copy in z_img:
                copy.wait_recv()

            @pl.when(no(last))
            def _():
                for copy in next_other:
                    copy.start()

    z_arrived(no(jnp.logical_or(outlet, beside)))
    turn(0)
    columns(1, 2)
    arrived(4)
    pass_on(both(inlet, no(zero)), 2)
    arrived(5)
    z_arrived(beside)
    turn(1)
    arrived(6, 7)
    pass_on(both(origin, behind), 3)
    columns(3, 4)
    arrived(8)
    pass_on(both(origin, no(behind)), 3)
    arrived(9)
    near = sorted([(5, part) for part in FAR[0]] + [(6, part) for part in FAR[1]])
    far = sorted([(5, part) for part in FAR[1]] + [(6, part) for part in FAR[0]])

    @pl.when(no(inlet))
    def _():
        image_arrived(2)
        image_arrived(3)

    @pl.when(origin)
    def _():
        image_arrived(2)

    turn(2)
    turn(3)
    arrived(10)
    columns(5, 6)
    scores(near)
    contribution(near)
    reduce_step(0, 1)
    scores(whole(0, 1, 2, 3, 4))
    arrived(11)
    scores(far)
    arrived(12)
    columns(7)
    opposite = sorted((7, part) for d in range(2) for part in FAR[d][:STEP])
    scores(opposite)
    contribution(opposite)
    reduce_step(2)
    contribution(whole(3, 4))
    contribution(far)
    arrived(13)
    opposite = sorted((7, part) for d in range(2) for part in FAR[d][STEP:])
    scores(opposite)
    contribution(opposite)
    @pl.when(lax.rem(b, 2) == 1)
    def _():
        g1[...] = image_term(1)

    reduce_step(3, 4)

    @pl.when(lax.rem(b, 2) == 0)
    def _():
        g1[...] = image_term(1)


    @pl.when(jnp.logical_not(inlet))
    def _():
        for j in (2, 3, 0, 1):
            gis[half(j), :] = g1[half(j), :].astype(BF16)
            back[j].start()

    @pl.when(jnp.logical_not(has_next))
    def _():
        gir[0 : 2 * ROWS, :] = jnp.zeros((2 * ROWS, gir.shape[1]), BF16)

    contribution(whole(1, 2))
    g0[...] = image_term(0)
    contribution(whole(0))
    reduce_step(5, 6, 7)
    inlet_back(no(zero), 0)
    inlet_back(no(zero), 1)
    reduce_step(8)
    own_back(no(last), 0, 1)
    reduce_step(9)
    inlet_back(no(zero), 2)
    reduce_step(10)
    inlet_back(no(zero), 3)
    reduce_step(11)
    own_back(last, 0)
    inlet_back(zero, 0)
    inlet_back(zero, 1)
    reduce_step(12, 13)
    inlet_back(zero, 2)
    inlet_back(zero, 3)
    own_back(last, 1)

    @pl.when(has_next)
    def _():
        back_wait(0)
        back_wait(1)

    for copy in z_own:
        copy.wait_recv()
    gi_out[0] = (scale * (g0[:ROWS, :] + gir[:ROWS, :].astype(F32) + zr[...].astype(F32))).astype(BF16)
    for part in sorted(range(PARTS), key=lambda part: r_orders[0].index((1, part)) + r_orders[1].index((1, part))):
        total = ct[part * CHUNK : (part + 1) * CHUNK, :]
        for d in range(2):
            m = r_orders[d].index((1, part))
            reduction[d][m].wait_recv()
            total = total + rrecv[d, m * CHUNK : (m + 1) * CHUNK, :].astype(F32)
        gt_out[0, part * CHUNK : (part + 1) * CHUNK, :] = (scale * total).astype(BF16)

    def all_sent(ref, sem):
        pltpu.make_async_copy(ref, ref, sem).wait()

    def images_sent(*sems):
        for sem in sems:
            all_sent(img.at[pl.ds(0, ROWS)], im_s.at[sem])
            all_sent(meta.at[0], me_s.at[sem])

    all_sent(rrecv, ag_s)
    all_sent(rrecv, rs_s)
    all_sent(col.at[pl.ds(0, 7)], co_s)
    all_sent(gis, gi_s)
    all_sent(zs, zz_s)
    images_sent(0)

    @pl.when(has_next)
    def _():
        images_sent(1, 2)

    @pl.when(inlet)
    def _():
        images_sent(3)

    @pl.when(both(inlet, no(zero)))
    def _():
        images_sent(4)

    @pl.when(direct_to)
    def _():
        images_sent(5)


def write(gi, gt, gi_out, gt_out, sems):
    copies = [
        pltpu.make_async_copy(src, dst, sems.at[i])
        for i, (src, dst) in enumerate(((gi, gi_out), (gt, gt_out)))
    ]
    for copy in copies:
        copy.start()
    for copy in copies:
        copy.wait()


def body(image, text, logit_scale, lse_row, lse_col, pair):
    width = image.shape[2]
    msgs = 3 * PARTS + PARTS // 2
    hbm = pl.BlockSpec(memory_space=pltpu.HBM)
    dma = pltpu.SemaphoreType.DMA
    vmem = pl.BlockSpec(memory_space=pltpu.VMEM)
    out = pltpu.VMEM((1, ROWS, width), BF16)
    grads = pl.pallas_call(
        kernel,
        out_shape=(out, out),
        in_specs=[hbm, hbm, pl.BlockSpec(memory_space=pltpu.SMEM), hbm, hbm, hbm],
        out_specs=(vmem, vmem),
        scratch_shapes=[
            pltpu.VMEM((PLACES * ROWS, width), BF16),
            pltpu.VMEM((4 * ROWS, width), BF16),
            pltpu.VMEM((width, 4 * ROWS), BF16),
            pltpu.VMEM((4, 8, ROWS), F32),
            pltpu.VMEM((PLACES, 8, ROWS), F32),
            pltpu.VMEM((PLACES * ROWS, ROWS), F32),
            pltpu.VMEM((PLACES * ROWS, 4 * ROWS), BF16),
            pltpu.VMEM((PLACES * ROWS, width), F32),
            pltpu.VMEM((2, msgs * CHUNK, width), BF16),
            pltpu.VMEM((2, msgs * CHUNK, width), BF16),
            pltpu.VMEM((2 * ROWS, width), F32),
            pltpu.VMEM((2 * ROWS, width), F32),
            pltpu.VMEM((2 * ROWS, width), BF16),
            pltpu.VMEM((4 * ROWS, width), BF16),
            pltpu.VMEM((ROWS, width), BF16),
            pltpu.VMEM((ROWS, width), BF16),
            pltpu.VMEM((2, 1, ROWS), BF16),
            pltpu.VMEM((1, ROWS), jnp.int32),
            pltpu.SemaphoreType.REGULAR((4,)),
            dma((5,)),
            dma,
            dma,
            dma((2, msgs)),
            dma((6,)),
            dma((6,)),
            dma((6,)),
            dma((3,)),
            dma,
            dma((2, 4)),
            dma,
            dma((8,)),
            dma,
            dma((2,)),
        ],
        compiler_params=pltpu.CompilerParams(
            collective_id=0, has_side_effects=True, vmem_limit_bytes=63 * 2**20
        ),
        cost_estimate=pl.CostEstimate(
            flops=12 * ROWS * 16 * ROWS * width, bytes_accessed=8 * ROWS * width, transcendentals=8 * ROWS * 16 * ROWS
        ),
    )(image, text, jnp.reshape(logit_scale, (1,)), lse_row, lse_col, pair)
    return pl.pallas_call(
        write,
        out_shape=[jax.ShapeDtypeStruct((1, ROWS, width), BF16)] * 2,
        in_specs=[vmem, vmem],
        out_specs=[hbm, hbm],
        scratch_shapes=[dma((2,))],
        compiler_params=pltpu.CompilerParams(vmem_limit_bytes=2**20),
    )(*grads)


def solution(mesh):
    return jax.shard_map(
        body,
        mesh=mesh,
        in_specs=(
            P("blk", "grp", None),
            P("blk", "grp", None),
            P(),
            P("blk", "grp"),
            P("blk", "grp"),
            P("blk", "grp"),
        ),
        out_specs=(P("blk", "grp", None), P("blk", "grp", None)),
        check_vma=False,
    )
```

```python
import functools

import jax
import jax.numpy as jnp
from jax import lax
from jax.experimental import pallas as pl
from jax.experimental.pallas import tpu as pltpu
from jax.sharding import PartitionSpec as P

MESH = pl.DeviceIdType.MESH
RING = 8
ROWS = 128
PARTS = 4
STEP = PARTS // 4
CHUNK = ROWS // PARTS
HALF = ROWS // 2
PLACES = 8
RUN = 8
FAR = ((2, 3), (1, 0))
F32 = jnp.float32
BF16 = jnp.bfloat16


def place(direction, hops):
    return 0 if hops == 0 else 7 if hops == 4 else 2 * hops - 1 + direction


def gather_order(direction):
    far, near = FAR[direction], FAR[1 - direction]
    order = [(hop, part) for hop in (1, 2, 3) for part in far + near]
    return order + [(4, part) for part in far]


def reduce_order(direction):
    f0, f1 = FAR[direction][:STEP], FAR[direction][STEP:]
    n0, n1 = FAR[1 - direction][:STEP], FAR[1 - direction][STEP:]
    order = [
        (3, n0), (3, n1), (4, f0), (4, f1), (2, n0), (3, f0), (3, f1),
        (2, n1), (2, f0), (2, f1), (1, n0), (1, n1), (1, f0), (1, f1),
    ]
    return [(hops, part) for hops, parts in order for part in parts]


def kernel(
    image, text, scale_ref, lrow_ref, lcol_ref, pair_ref, gi_out, gt_out,
    txt, img, imgt, meta, col, lct, dt, ct, rsend, rrecv, g0, g1, gis, gir, zs, zr, vecs, pairs,
    ready, local_sem, ag_s, rs_s, ring_r, im_s, im_r, me_s, me_r, co_s, co_r, gi_s, gi_r, zz_s, zz_r,
):
    g = lax.axis_index("grp")
    b = lax.axis_index("blk")
    n_blk = lax.axis_size("blk")
    n_grp = 2 * RING
    zpart = g + 1 - 2 * lax.rem(g, 2)
    nxt = lax.rem(b + 1, n_blk)
    prv = lax.rem(b + n_blk - 1, n_blk)
    ring = [lax.rem(g + 2 * i, n_grp) for i in range(RING)]
    side = [ring[1], ring[7]]
    z_lo = lax.rem(g, 2)
    last = lax.rem(b, RUN) == RUN - 1
    first = lax.rem(b, RUN) == 0
    zero = b == 0
    low, high = z_lo == 0, z_lo == 1
    no = jnp.logical_not
    both = jnp.logical_and
    has_next = no(both(last, low))
    has_prev = no(both(first, high))
    outlet = both(last, high)
    inlet = both(first, low)
    next_grp = jnp.where(last, zpart, g)
    prev_grp = jnp.where(first, zpart, g)

    y = g // 2
    origin = both(zero, low)
    left_first = jnp.where(y == 0, origin, both(y < 7, no(both(origin, y == 1))))
    right_first = jnp.where(y == 0, origin, jnp.where(y == 7, no(origin), y == 6))
    z_first = jnp.where(jnp.logical_or(both(zero, y == 0), nxt == 0), low, high)
    early = lambda blk: jnp.logical_or(blk == 0, blk == n_blk - RUN)
    prev_first = both(has_prev, no(jnp.logical_or(early(b), both(b == 1, both(y == 0, low)))))
    next_first = both(has_next, jnp.logical_or(early(nxt), both(origin, y == 0)))
    direct_from = both(zero, high)
    direct_to = both(nxt == 0, low)
    meets = (
        (left_first, True, side[1], b, 1),
        (right_first, True, side[0], b, 0),
        (z_first, True, zpart, b, 2),
        (prev_first, has_prev, prev_grp, prv, 3),
        (next_first, has_next, next_grp, nxt, None),
        (direct_to, direct_from, zpart, prv, None),
    )
    barrier = pltpu.get_barrier_semaphore()

    def greet(grp, blk, sem):
        pl.semaphore_signal(sem, inc=1, device_id={"grp": grp, "blk": blk}, device_id_type=MESH)

    for they_first, met, grp, blk, _ in meets:

        @pl.when(both(met, no(they_first)))
        def _(grp=grp, blk=blk):
            greet(grp, blk, barrier)

    def copy_to(src, dst, s_sem, r_sem, grp=g, blk=b):
        return pltpu.make_async_remote_copy(
            src_ref=src, dst_ref=dst, send_sem=s_sem, recv_sem=r_sem,
            device_id={"grp": grp, "blk": blk}, device_id_type=MESH,
        )

    local = [
        pltpu.make_async_copy(src, dst, local_sem.at[i])
        for i, (src, dst) in enumerate((
            (pair_ref, pairs),
            (lrow_ref, vecs.at[0]),
            (lcol_ref, vecs.at[1]),
            (text.at[0], txt.at[pl.ds(0, ROWS)]),
            (image.at[0], img.at[pl.ds(0, ROWS)]),
        ))
    ]
    for copy in local:
        copy.start()
    scale = scale_ref[0]

    def go(copy):
        copy.start()

    orders = [gather_order(0), gather_order(1)]

    def gather_copy(direction, n):
        hop, part = orders[direction][n]
        rows = lambda p: txt.at[pl.ds(p * ROWS + part * CHUNK, CHUNK)]
        src = text.at[0, pl.ds(part * CHUNK, CHUNK)] if hop == 1 else rows(place(direction, hop - 1))
        return copy_to(
            src, rows(place(direction, hop)), ag_s, ring_r.at[direction, n], grp=side[direction]
        )

    def col_copy(direction, hop):
        return copy_to(
            col.at[place(direction, hop - 1)], col.at[place(direction, hop)],
            co_s, co_r.at[direction, hop - 1], grp=side[direction],
        )

    gather = [[gather_copy(d, n) for n in range(len(orders[d]))] for d in range(2)]
    cols = [[col_copy(0, hop) for hop in (1, 2, 3, 4)], [col_copy(1, hop) for hop in (1, 2, 3)]]

    def arrived(*steps):
        for n in [STEP * step + i for step in steps for i in range(STEP)]:
            hop = n // PARTS + 1
            for d in range(2):
                if n % PARTS == 0 and hop <= len(cols[d]):
                    cols[d][hop - 1].wait_recv()
                    if hop < len(cols[d]):
                        go(cols[d][hop])
                gather[d][n].wait_recv()
                if n + PARTS < len(orders[d]):
                    go(gather[d][n + PARTS])

    def image_copies(src, dst, sem, **to):
        def copy(i):
            start = i * HALF
            rows = image.at[0, pl.ds(start, HALF)] if src == 0 else img.at[pl.ds(src * ROWS + start, HALF)]
            r_sem = im_r.at[2 * (dst - 1) + i]
            return copy_to(rows, img.at[pl.ds(dst * ROWS + start, HALF)], im_s.at[sem], r_sem, **to)

        return copy(0), copy(1), copy_to(meta.at[src], meta.at[dst], me_s.at[sem], me_r.at[dst - 1], **to)

    swap = last.astype(jnp.int32)
    z_img = image_copies(0, 1, 0, grp=zpart)
    next_own = image_copies(0, 2 + swap, 1, grp=next_grp, blk=nxt)
    next_other = image_copies(1, 3 - swap, 2, grp=next_grp, blk=nxt)
    passed = {3: image_copies(3, 2, 3, grp=zpart), 2: image_copies(2, 3, 4, grp=zpart)}
    direct = image_copies(0, 3, 5, grp=zpart, blk=nxt)
    arrivals = {2: image_copies(0, 2, 0, grp=zpart), 3: image_copies(0, 3, 0, grp=zpart)}

    def image_arrived(slot):
        for copy in arrivals[slot]:
            copy.wait_recv()

    def start_if(condition, copies):
        @pl.when(condition)
        def _():
            for copy in copies:
                copy.start()

    def pass_on(condition, slot):
        @pl.when(condition)
        def _():
            for got, copy in zip(arrivals[slot], passed[slot]):
                got.wait_recv()
                copy.start()

    def take(ref, parts):
        pieces = []
        for p, part in parts:
            lo = p * ROWS + part * CHUNK
            if pieces and pieces[-1][1] == lo:
                pieces[-1][1] = lo + CHUNK
            else:
                pieces.append([lo, lo + CHUNK])
        pieces = [ref[lo:hi, :] for lo, hi in pieces]
        return pieces[0] if len(pieces) == 1 else jnp.concatenate(pieces, axis=0)

    def whole(*places):
        return [(p, part) for p in places for part in range(PARTS)]

    def columns(*places):
        for p in places:
            lct[p * ROWS : (p + 1) * ROWS, :] = jnp.broadcast_to(col[p, 0:1, :], (ROWS, ROWS)).T

    def turn(slot):
        imgt[:, slot * ROWS : (slot + 1) * ROWS] = img[slot * ROWS : (slot + 1) * ROWS, :].T

    def scores(parts):
        s = jnp.dot(take(txt, parts), imgt[...], preferred_element_type=F32) * scale
        lr = jnp.concatenate([meta[slot, 0:1, :] for slot in range(4)], axis=1)
        lc = take(lct, parts)
        d = 0.5 * (jnp.exp(s - lr) + jnp.exp(s - jnp.concatenate([lc] * 4, axis=1)))
        pr = jnp.concatenate([meta[0, 1:2, :], meta[1, 1:2, :]], axis=1).astype(jnp.int32)
        iota = lax.broadcasted_iota(jnp.int32, (CHUNK, 2 * ROWS), 0)
        for i, (p, part) in enumerate(parts):
            rel = 0 if p == 0 else 4 if p == 7 else (RING - (p + 1) // 2) if p % 2 else p // 2
            rows = d[i * CHUNK : (i + 1) * CHUNK]
            own = rows[:, : 2 * ROWS] - (pr - (ring[rel] * ROWS + part * CHUNK) == iota).astype(F32)
            lo = p * ROWS + part * CHUNK
            dt[lo : lo + CHUNK, : 2 * ROWS] = own.astype(BF16)
            dt[lo : lo + CHUNK, 2 * ROWS :] = rows[:, 2 * ROWS :].astype(BF16)

    def contribution(parts):
        c = jnp.dot(take(dt, parts), img[...], preferred_element_type=F32)
        for i, (p, part) in enumerate(parts):
            lo = p * ROWS + part * CHUNK
            ct[lo : lo + CHUNK, :] = c[i * CHUNK : (i + 1) * CHUNK]

    def image_term(k):
        return lax.dot_general(
            dt[:, k * 2 * ROWS : (k + 1) * 2 * ROWS], txt[...], (((0,), (0,)), ((), ())), preferred_element_type=F32
        )

    r_orders = [reduce_order(0), reduce_order(1)]

    def reduce_copy(direction, n):
        rows = pl.ds(n * CHUNK, CHUNK)
        return copy_to(
            rsend.at[direction, rows], rrecv.at[direction, rows],
            rs_s, ring_r.at[direction, n], grp=side[direction],
        )

    reduction = [[reduce_copy(d, n) for n in range(len(r_orders[d]))] for d in range(2)]

    def reduce_step(*steps):
        for n in [STEP * step + i for step in steps for i in range(STEP)]:
            for d in range(2):
                hops, part = r_orders[d][n]
                start = place(1 - d, hops) * ROWS + part * CHUNK
                total = ct[start : start + CHUNK, :]
                if (hops + 1, part) in r_orders[d]:
                    m = r_orders[d].index((hops + 1, part))
                    reduction[d][m].wait_recv()
                    total = total + rrecv[d, m * CHUNK : (m + 1) * CHUNK, :].astype(F32)
                rsend[d, n * CHUNK : (n + 1) * CHUNK, :] = total.astype(BF16)
                go(reduction[d][n])

    half = lambda j: slice(j * HALF, (j + 1) * HALF)
    feeder = jnp.logical_and(first, z_lo == 1)
    back_blk = jnp.where(feeder, b, prv)

    def back_copy(j):
        if j < 2:
            to = jnp.where(feeder, j + 6, jnp.where(inlet, j + 2, j))
        else:
            to = jnp.where(feeder, j + 2, jnp.where(inlet, j - 2, j))
        return copy_to(
            gis.at[pl.ds(j * HALF, HALF)], gir.at[pl.ds(pl.multiple_of(to * HALF, HALF), HALF)],
            gi_s, gi_r.at[to], grp=prev_grp, blk=back_blk,
        )

    back = [back_copy(j) for j in range(4)]

    def back_wait(to):
        rows = pl.ds(to * HALF, HALF)
        copy_to(gis.at[pl.ds(0, HALF)], gir.at[rows], gi_s, gi_r.at[to], grp=zpart).wait_recv()

    def inlet_back(condition, j):
        @pl.when(both(inlet, condition))
        def _():
            back_wait(4 + j)
            gis[half(j), :] = (g1[half(j), :] + gir[half(4 + j), :].astype(F32)).astype(BF16)
            back[j].start()

    z_own = [
        copy_to(zs.at[pl.ds(i * HALF, HALF)], zr.at[pl.ds(i * HALF, HALF)], zz_s, zz_r.at[i], grp=zpart)
        for i in range(2)
    ]

    def own_back(condition, *halves):
        @pl.when(condition)
        def _():
            for i in halves:

                @pl.when(has_next)
                def _():
                    back_wait(2 + i)

                zs[half(i), :] = (g0[half(2 + i), :] + gir[half(2 + i), :].astype(F32)).astype(BF16)
                z_own[i].start()

    behind = jnp.logical_or(y < 2, y == RING - 1)

    greeted = sum(they_first.astype(jnp.int32) for they_first, *_ in meets)

    @pl.when(greeted > 0)
    def _():
        pl.semaphore_wait(barrier, greeted)

    for they_first, _, grp, blk, sem in meets:
        if sem is not None:

            @pl.when(they_first)
            def _(grp=grp, blk=blk, sem=sem):
                greet(grp, blk, ready.at[sem])

    for copy in local[:3]:
        copy.wait()
    meta[0] = jnp.zeros((8, ROWS), F32)
    meta[0, 0:1, :] = vecs[0].astype(F32)
    meta[0, 1:2, :] = pairs[...].astype(F32)
    col[0] = jnp.broadcast_to(vecs[1].astype(F32), (8, ROWS))

    def open_side(condition, d, answer):
        @pl.when(condition)
        def _():
            if answer:
                pl.semaphore_wait(ready.at[1 - d], 1)
            cols[d][0].start()
            for n in range(PARTS):
                gather[d][n].start()

    open_side(left_first, 1, False)
    open_side(right_first, 0, False)
    beside = lax.rem(b, RUN) == RUN - 2
    held = jnp.logical_or(beside, both(both(zero, y == 0), high))

    def open_z(condition):
        @pl.when(condition)
        def _():
            @pl.when(no(z_first))
            def _():
                pl.semaphore_wait(ready.at[2], 1)

            for copy in z_img:
                copy.start()

    open_z(last)

    def open_next(condition):
        @pl.when(both(has_next, condition))
        def _():
            @pl.when(no(next_first))
            def _():
                pl.semaphore_wait(ready.at[3], 1)

            for copy in next_own:
                copy.start()

    open_next(next_first)
    open_side(no(right_first), 0, True)
    open_side(no(left_first), 1, True)
    open_z(no(jnp.logical_or(held, last)))

    open_next(no(next_first))
    for copy in local[3:]:
        copy.wait()
    columns(0)
    arrived(0)
    start_if(direct_to, direct)

    @pl.when(outlet)
    def _():
        z_img[0].wait_recv()
        next_other[0].start()

    arrived(1)
    open_z(held)

    @pl.when(outlet)
    def _():
        for got, copy in zip(z_img[1:], next_other[1:]):
            got.wait_recv()
            copy.start()

    arrived(2)
    pass_on(both(inlet, no(zero)), 3)
    arrived(3)

    def z_arrived(condition):
        @pl.when(condition)
        def _():
            for copy in z_img:
                copy.wait_recv()

            @pl.when(no(last))
            def _():
                for copy in next_other:
                    copy.start()

    z_arrived(no(jnp.logical_or(outlet, beside)))
    turn(0)
    columns(1, 2)
    arrived(4)
    pass_on(both(inlet, no(zero)), 2)
    arrived(5)
    z_arrived(beside)
    turn(1)
    arrived(6)
    pass_on(both(origin, behind), 3)
    arrived(7)
    pass_on(both(origin, no(behind)), 3)
    columns(3, 4)
    arrived(8, 9)
    near = sorted([(5, part) for part in FAR[0]] + [(6, part) for part in FAR[1]])
    far = sorted([(5, part) for part in FAR[1]] + [(6, part) for part in FAR[0]])

    @pl.when(no(inlet))
    def _():
        image_arrived(2)
        image_arrived(3)

    @pl.when(origin)
    def _():
        image_arrived(2)

    turn(2)
    turn(3)
    arrived(10)
    columns(5, 6)
    scores(near)
    contribution(near)
    reduce_step(0, 1)
    scores(whole(0, 1, 2, 3, 4))
    arrived(11)
    scores(far)
    arrived(12)
    columns(7)
    opposite = sorted((7, part) for d in range(2) for part in FAR[d][:STEP])
    scores(opposite)
    contribution(opposite)
    reduce_step(2)
    contribution(whole(3, 4))
    contribution(far)
    arrived(13)
    opposite = sorted((7, part) for d in range(2) for part in FAR[d][STEP:])
    scores(opposite)
    contribution(opposite)
    @pl.when(lax.rem(b, 2) == 1)
    def _():
        g1[...] = image_term(1)

    reduce_step(3, 4)

    @pl.when(lax.rem(b, 2) == 0)
    def _():
        g1[...] = image_term(1)


    @pl.when(jnp.logical_not(inlet))
    def _():
        for j in (2, 3, 0, 1):
            gis[half(j), :] = g1[half(j), :].astype(BF16)
            back[j].start()

    @pl.when(jnp.logical_not(has_next))
    def _():
        gir[0 : 2 * ROWS, :] = jnp.zeros((2 * ROWS, gir.shape[1]), BF16)

    contribution(whole(1, 2))
    g0[...] = image_term(0)
    contribution(whole(0))
    reduce_step(5, 6, 7)
    inlet_back(no(zero), 0)
    inlet_back(no(zero), 1)
    reduce_step(8)
    own_back(no(last), 0, 1)
    reduce_step(9)
    inlet_back(no(zero), 2)
    reduce_step(10)
    inlet_back(no(zero), 3)
    reduce_step(11)
    own_back(last, 0)
    inlet_back(zero, 0)
    inlet_back(zero, 1)
    reduce_step(12, 13)
    inlet_back(zero, 2)
    inlet_back(zero, 3)
    own_back(last, 1)

    @pl.when(has_next)
    def _():
        back_wait(0)
        back_wait(1)

    for copy in z_own:
        copy.wait_recv()
    gi_out[0] = (scale * (g0[:ROWS, :] + gir[:ROWS, :].astype(F32) + zr[...].astype(F32))).astype(BF16)
    for part in sorted(range(PARTS), key=lambda part: r_orders[0].index((1, part)) + r_orders[1].index((1, part))):
        total = ct[part * CHUNK : (part + 1) * CHUNK, :]
        for d in range(2):
            m = r_orders[d].index((1, part))
            reduction[d][m].wait_recv()
            total = total + rrecv[d, m * CHUNK : (m + 1) * CHUNK, :].astype(F32)
        gt_out[0, part * CHUNK : (part + 1) * CHUNK, :] = (scale * total).astype(BF16)

    def all_sent(ref, sem):
        pltpu.make_async_copy(ref, ref, sem).wait()

    def images_sent(*sems):
        for sem in sems:
            all_sent(img.at[pl.ds(0, ROWS)], im_s.at[sem])
            all_sent(meta.at[0], me_s.at[sem])

    all_sent(rrecv, ag_s)
    all_sent(rrecv, rs_s)
    all_sent(col.at[pl.ds(0, 7)], co_s)
    all_sent(gis, gi_s)
    all_sent(zs, zz_s)
    images_sent(0)

    @pl.when(has_next)
    def _():
        images_sent(1, 2)

    @pl.when(inlet)
    def _():
        images_sent(3)

    @pl.when(both(inlet, no(zero)))
    def _():
        images_sent(4)

    @pl.when(direct_to)
    def _():
        images_sent(5)


def write(gi, gt, gi_out, gt_out, sems):
    copies = [
        pltpu.make_async_copy(src, dst, sems.at[i])
        for i, (src, dst) in enumerate(((gi, gi_out), (gt, gt_out)))
    ]
    for copy in copies:
        copy.start()
    for copy in copies:
        copy.wait()


def body(image, text, logit_scale, lse_row, lse_col, pair):
    width = image.shape[2]
    msgs = 3 * PARTS + PARTS // 2
    hbm = pl.BlockSpec(memory_space=pltpu.HBM)
    dma = pltpu.SemaphoreType.DMA
    vmem = pl.BlockSpec(memory_space=pltpu.VMEM)
    out = pltpu.VMEM((1, ROWS, width), BF16)
    grads = pl.pallas_call(
        kernel,
        out_shape=(out, out),
        in_specs=[hbm, hbm, pl.BlockSpec(memory_space=pltpu.SMEM), hbm, hbm, hbm],
        out_specs=(vmem, vmem),
        scratch_shapes=[
            pltpu.VMEM((PLACES * ROWS, width), BF16),
            pltpu.VMEM((4 * ROWS, width), BF16),
            pltpu.VMEM((width, 4 * ROWS), BF16),
            pltpu.VMEM((4, 8, ROWS), F32),
            pltpu.VMEM((PLACES, 8, ROWS), F32),
            pltpu.VMEM((PLACES * ROWS, ROWS), F32),
            pltpu.VMEM((PLACES * ROWS, 4 * ROWS), BF16),
            pltpu.VMEM((PLACES * ROWS, width), F32),
            pltpu.VMEM((2, msgs * CHUNK, width), BF16),
            pltpu.VMEM((2, msgs * CHUNK, width), BF16),
            pltpu.VMEM((2 * ROWS, width), F32),
            pltpu.VMEM((2 * ROWS, width), F32),
            pltpu.VMEM((2 * ROWS, width), BF16),
            pltpu.VMEM((4 * ROWS, width), BF16),
            pltpu.VMEM((ROWS, width), BF16),
            pltpu.VMEM((ROWS, width), BF16),
            pltpu.VMEM((2, 1, ROWS), BF16),
            pltpu.VMEM((1, ROWS), jnp.int32),
            pltpu.SemaphoreType.REGULAR((4,)),
            dma((5,)),
            dma,
            dma,
            dma((2, msgs)),
            dma((6,)),
            dma((6,)),
            dma((6,)),
            dma((3,)),
            dma,
            dma((2, 4)),
            dma,
            dma((8,)),
            dma,
            dma((2,)),
        ],
        compiler_params=pltpu.CompilerParams(
            collective_id=0, has_side_effects=True, vmem_limit_bytes=63 * 2**20
        ),
        cost_estimate=pl.CostEstimate(
            flops=12 * ROWS * 16 * ROWS * width, bytes_accessed=8 * ROWS * width, transcendentals=8 * ROWS * 16 * ROWS
        ),
    )(image, text, jnp.reshape(logit_scale, (1,)), lse_row, lse_col, pair)
    return pl.pallas_call(
        write,
        out_shape=[jax.ShapeDtypeStruct((1, ROWS, width), BF16)] * 2,
        in_specs=[vmem, vmem],
        out_specs=[hbm, hbm],
        scratch_shapes=[dma((2,))],
        compiler_params=pltpu.CompilerParams(vmem_limit_bytes=2**20),
    )(*grads)


def solution(mesh):
    return jax.shard_map(
        body,
        mesh=mesh,
        in_specs=(
            P("blk", "grp", None),
            P("blk", "grp", None),
            P(),
            P("blk", "grp"),
            P("blk", "grp"),
            P("blk", "grp"),
        ),
        out_specs=(P("blk", "grp", None), P("blk", "grp", None)),
        check_vma=False,
    )
```

```python
import functools

import jax
import jax.numpy as jnp
from jax import lax
from jax.experimental import pallas as pl
from jax.experimental.pallas import tpu as pltpu
from jax.sharding import PartitionSpec as P

MESH = pl.DeviceIdType.MESH
RING = 8
ROWS = 128
PARTS = 4
STEP = PARTS // 4
CHUNK = ROWS // PARTS
HALF = ROWS // 2
PLACES = 8
RUN = 8
FAR = ((2, 3), (1, 0))
F32 = jnp.float32
BF16 = jnp.bfloat16


def place(direction, hops):
    return 0 if hops == 0 else 7 if hops == 4 else 2 * hops - 1 + direction


def gather_order(direction):
    far, near = FAR[direction], FAR[1 - direction]
    order = [(hop, part) for hop in (1, 2, 3) for part in far + near]
    return order + [(4, part) for part in far]


def reduce_order(direction):
    f0, f1 = FAR[direction][:STEP], FAR[direction][STEP:]
    n0, n1 = FAR[1 - direction][:STEP], FAR[1 - direction][STEP:]
    order = [
        (3, n0), (3, n1), (4, f0), (4, f1), (2, n0), (3, f0), (3, f1),
        (2, n1), (2, f0), (2, f1), (1, n0), (1, n1), (1, f0), (1, f1),
    ]
    return [(hops, part) for hops, parts in order for part in parts]


def kernel(
    image, text, scale_ref, lrow_ref, lcol_ref, pair_ref, gi_out, gt_out,
    txt, img, imgt, meta, col, lct, dt, ct, rsend, rrecv, g0, g1, gis, gir, zs, zr, vecs, pairs,
    ready, local_sem, ag_s, rs_s, ring_r, im_s, im_r, me_s, me_r, co_s, co_r, gi_s, gi_r, zz_s, zz_r,
):
    g = lax.axis_index("grp")
    b = lax.axis_index("blk")
    n_blk = lax.axis_size("blk")
    n_grp = 2 * RING
    zpart = g + 1 - 2 * lax.rem(g, 2)
    nxt = lax.rem(b + 1, n_blk)
    prv = lax.rem(b + n_blk - 1, n_blk)
    ring = [lax.rem(g + 2 * i, n_grp) for i in range(RING)]
    side = [ring[1], ring[7]]
    z_lo = lax.rem(g, 2)
    last = lax.rem(b, RUN) == RUN - 1
    first = lax.rem(b, RUN) == 0
    zero = b == 0
    low, high = z_lo == 0, z_lo == 1
    no = jnp.logical_not
    both = jnp.logical_and
    has_next = no(both(last, low))
    has_prev = no(both(first, high))
    outlet = both(last, high)
    inlet = both(first, low)
    next_grp = jnp.where(last, zpart, g)
    prev_grp = jnp.where(first, zpart, g)

    y = g // 2
    origin = both(zero, low)
    left_first = jnp.where(y == 0, origin, both(y < 7, no(both(origin, y == 1))))
    right_first = jnp.where(y == 0, origin, jnp.where(y == 7, no(origin), y == 6))
    z_first = jnp.where(jnp.logical_or(both(zero, y == 0), nxt == 0), low, high)
    early = lambda blk: jnp.logical_or(blk == 0, blk == n_blk - RUN)
    prev_first = both(has_prev, no(jnp.logical_or(early(b), both(b == 1, both(y == 0, low)))))
    next_first = both(has_next, jnp.logical_or(early(nxt), both(origin, y == 0)))
    direct_from = both(zero, high)
    direct_to = both(nxt == 0, low)
    meets = (
        (left_first, True, side[1], b, 1),
        (right_first, True, side[0], b, 0),
        (z_first, True, zpart, b, 2),
        (prev_first, has_prev, prev_grp, prv, 3),
        (next_first, has_next, next_grp, nxt, None),
        (direct_to, direct_from, zpart, prv, None),
    )
    barrier = pltpu.get_barrier_semaphore()

    def greet(grp, blk, sem):
        pl.semaphore_signal(sem, inc=1, device_id={"grp": grp, "blk": blk}, device_id_type=MESH)

    for they_first, met, grp, blk, _ in meets:

        @pl.when(both(met, no(they_first)))
        def _(grp=grp, blk=blk):
            greet(grp, blk, barrier)

    def copy_to(src, dst, s_sem, r_sem, grp=g, blk=b):
        return pltpu.make_async_remote_copy(
            src_ref=src, dst_ref=dst, send_sem=s_sem, recv_sem=r_sem,
            device_id={"grp": grp, "blk": blk}, device_id_type=MESH,
        )

    local = [
        pltpu.make_async_copy(src, dst, local_sem.at[min(i, 3)])
        for i, (src, dst) in enumerate((
            (pair_ref, pairs),
            (lrow_ref, vecs.at[0]),
            (lcol_ref, vecs.at[1]),
            (text.at[0], txt.at[pl.ds(0, ROWS)]),
            (image.at[0], img.at[pl.ds(0, ROWS)]),
        ))
    ]
    for copy in local:
        copy.start()
    scale = scale_ref[0]

    def go(copy):
        copy.start()

    orders = [gather_order(0), gather_order(1)]

    def gather_copy(direction, n):
        hop, part = orders[direction][n]
        rows = lambda p: txt.at[pl.ds(p * ROWS + part * CHUNK, CHUNK)]
        src = text.at[0, pl.ds(part * CHUNK, CHUNK)] if hop == 1 else rows(place(direction, hop - 1))
        return copy_to(
            src, rows(place(direction, hop)), ag_s, ring_r.at[direction, n], grp=side[direction]
        )

    def col_copy(direction, hop):
        return copy_to(
            col.at[place(direction, hop - 1)], col.at[place(direction, hop)],
            co_s, co_r.at[direction, hop - 1], grp=side[direction],
        )

    gather = [[gather_copy(d, n) for n in range(len(orders[d]))] for d in range(2)]
    cols = [[col_copy(0, hop) for hop in (1, 2, 3, 4)], [col_copy(1, hop) for hop in (1, 2, 3)]]

    def arrived(*steps):
        for n in [STEP * step + i for step in steps for i in range(STEP)]:
            hop = n // PARTS + 1
            for d in range(2):
                if n % PARTS == 0 and hop <= len(cols[d]):
                    cols[d][hop - 1].wait_recv()
                    if hop < len(cols[d]):
                        go(cols[d][hop])
                gather[d][n].wait_recv()
                if n + PARTS < len(orders[d]):
                    go(gather[d][n + PARTS])

    def image_copies(src, dst, **to):
        def copy(i):
            start = i * HALF
            rows = image.at[0, pl.ds(start, HALF)] if src == 0 else img.at[pl.ds(src * ROWS + start, HALF)]
            r_sem = im_r.at[2 * (dst - 1) + i]
            return copy_to(rows, img.at[pl.ds(dst * ROWS + start, HALF)], im_s, r_sem, **to)

        return copy(0), copy(1), copy_to(meta.at[src], meta.at[dst], me_s, me_r.at[dst - 1], **to)

    swap = last.astype(jnp.int32)
    z_img = image_copies(0, 1, grp=zpart)
    next_own = image_copies(0, 2 + swap, grp=next_grp, blk=nxt)
    next_other = image_copies(1, 3 - swap, grp=next_grp, blk=nxt)
    passed = {3: image_copies(3, 2, grp=zpart), 2: image_copies(2, 3, grp=zpart)}
    direct = image_copies(0, 3, grp=zpart, blk=nxt)
    arrivals = {2: image_copies(0, 2, grp=zpart), 3: image_copies(0, 3, grp=zpart)}

    def image_arrived(slot):
        for copy in arrivals[slot]:
            copy.wait_recv()

    def start_if(condition, copies):
        @pl.when(condition)
        def _():
            for copy in copies:
                copy.start()

    def pass_on(condition, slot):
        @pl.when(condition)
        def _():
            for got, copy in zip(arrivals[slot], passed[slot]):
                got.wait_recv()
                copy.start()

    def take(ref, parts):
        pieces = []
        for p, part in parts:
            lo = p * ROWS + part * CHUNK
            if pieces and pieces[-1][1] == lo:
                pieces[-1][1] = lo + CHUNK
            else:
                pieces.append([lo, lo + CHUNK])
        pieces = [ref[lo:hi, :] for lo, hi in pieces]
        return pieces[0] if len(pieces) == 1 else jnp.concatenate(pieces, axis=0)

    def whole(*places):
        return [(p, part) for p in places for part in range(PARTS)]

    def columns(*places):
        for p in places:
            lct[p * ROWS : (p + 1) * ROWS, :] = jnp.broadcast_to(col[p, 0:1, :], (ROWS, ROWS)).T

    def turn(slot):
        imgt[:, slot * ROWS : (slot + 1) * ROWS] = img[slot * ROWS : (slot + 1) * ROWS, :].T

    def scores(parts):
        s = jnp.dot(take(txt, parts), imgt[...], preferred_element_type=F32) * scale
        lr = jnp.concatenate([meta[slot, 0:1, :] for slot in range(4)], axis=1)
        lc = take(lct, parts)
        d = 0.5 * (jnp.exp(s - lr) + jnp.exp(s - jnp.concatenate([lc] * 4, axis=1)))
        pr = jnp.concatenate([meta[0, 1:2, :], meta[1, 1:2, :]], axis=1).astype(jnp.int32)
        iota = lax.broadcasted_iota(jnp.int32, (CHUNK, 2 * ROWS), 0)
        for i, (p, part) in enumerate(parts):
            rel = 0 if p == 0 else 4 if p == 7 else (RING - (p + 1) // 2) if p % 2 else p // 2
            rows = d[i * CHUNK : (i + 1) * CHUNK]
            own = rows[:, : 2 * ROWS] - (pr - (ring[rel] * ROWS + part * CHUNK) == iota).astype(F32)
            lo = p * ROWS + part * CHUNK
            dt[lo : lo + CHUNK, : 2 * ROWS] = own.astype(BF16)
            dt[lo : lo + CHUNK, 2 * ROWS :] = rows[:, 2 * ROWS :].astype(BF16)

    def contribution(parts):
        c = jnp.dot(take(dt, parts), img[...], preferred_element_type=F32)
        for i, (p, part) in enumerate(parts):
            lo = p * ROWS + part * CHUNK
            ct[lo : lo + CHUNK, :] = c[i * CHUNK : (i + 1) * CHUNK]

    def image_term(k):
        return lax.dot_general(
            dt[:, k * 2 * ROWS : (k + 1) * 2 * ROWS], txt[...], (((0,), (0,)), ((), ())), preferred_element_type=F32
        )

    r_orders = [reduce_order(0), reduce_order(1)]

    def reduce_copy(direction, n):
        rows = pl.ds(n * CHUNK, CHUNK)
        return copy_to(
            rsend.at[direction, rows], rrecv.at[direction, rows],
            rs_s, ring_r.at[direction, n], grp=side[direction],
        )

    reduction = [[reduce_copy(d, n) for n in range(len(r_orders[d]))] for d in range(2)]

    def reduce_step(*steps):
        for n in [STEP * step + i for step in steps for i in range(STEP)]:
            for d in range(2):
                hops, part = r_orders[d][n]
                start = place(1 - d, hops) * ROWS + part * CHUNK
                total = ct[start : start + CHUNK, :]
                if (hops + 1, part) in r_orders[d]:
                    m = r_orders[d].index((hops + 1, part))
                    reduction[d][m].wait_recv()
                    total = total + rrecv[d, m * CHUNK : (m + 1) * CHUNK, :].astype(F32)
                rsend[d, n * CHUNK : (n + 1) * CHUNK, :] = total.astype(BF16)
                go(reduction[d][n])

    half = lambda j: slice(j * HALF, (j + 1) * HALF)
    feeder = jnp.logical_and(first, z_lo == 1)
    back_blk = jnp.where(feeder, b, prv)

    def back_copy(j):
        if j < 2:
            to = jnp.where(feeder, j + 6, jnp.where(inlet, j + 2, j))
        else:
            to = jnp.where(feeder, j + 2, jnp.where(inlet, j - 2, j))
        return copy_to(
            gis.at[pl.ds(j * HALF, HALF)], gir.at[pl.ds(pl.multiple_of(to * HALF, HALF), HALF)],
            gi_s, gi_r.at[to], grp=prev_grp, blk=back_blk,
        )

    back = [back_copy(j) for j in range(4)]

    def back_wait(to):
        rows = pl.ds(to * HALF, HALF)
        copy_to(gis.at[pl.ds(0, HALF)], gir.at[rows], gi_s, gi_r.at[to], grp=zpart).wait_recv()

    def inlet_back(condition, j):
        @pl.when(both(inlet, condition))
        def _():
            back_wait(4 + j)
            gis[half(j), :] = (g1[half(j), :] + gir[half(4 + j), :].astype(F32)).astype(BF16)
            back[j].start()

    z_own = [
        copy_to(zs.at[pl.ds(i * HALF, HALF)], zr.at[pl.ds(i * HALF, HALF)], zz_s, zz_r.at[i], grp=zpart)
        for i in range(2)
    ]

    def own_back(condition, *halves):
        @pl.when(condition)
        def _():
            for i in halves:

                @pl.when(has_next)
                def _():
                    back_wait(2 + i)

                zs[half(i), :] = (g0[half(2 + i), :] + gir[half(2 + i), :].astype(F32)).astype(BF16)
                z_own[i].start()

    behind = jnp.logical_or(y < 2, y == RING - 1)

    greeted = sum(they_first.astype(jnp.int32) for they_first, *_ in meets)

    @pl.when(greeted > 0)
    def _():
        pl.semaphore_wait(barrier, greeted)

    for they_first, _, grp, blk, sem in meets:
        if sem is not None:

            @pl.when(they_first)
            def _(grp=grp, blk=blk, sem=sem):
                greet(grp, blk, ready.at[sem])

    for copy in local[:3]:
        copy.wait()
    meta[0] = jnp.zeros((8, ROWS), F32)
    meta[0, 0:1, :] = vecs[0].astype(F32)
    meta[0, 1:2, :] = pairs[...].astype(F32)
    col[0] = jnp.broadcast_to(vecs[1].astype(F32), (8, ROWS))

    def open_side(condition, d, answer):
        @pl.when(condition)
        def _():
            if answer:
                pl.semaphore_wait(ready.at[1 - d], 1)
            cols[d][0].start()
            for n in range(PARTS):
                gather[d][n].start()

    open_side(left_first, 1, False)
    open_side(right_first, 0, False)
    beside = lax.rem(b, RUN) == RUN - 2
    held = jnp.logical_or(beside, both(both(zero, y == 0), high))

    def open_z(condition):
        @pl.when(condition)
        def _():
            @pl.when(no(z_first))
            def _():
                pl.semaphore_wait(ready.at[2], 1)

            for copy in z_img:
                copy.start()

    open_z(last)

    def open_next(condition):
        @pl.when(both(has_next, condition))
        def _():
            @pl.when(no(next_first))
            def _():
                pl.semaphore_wait(ready.at[3], 1)

            for copy in next_own:
                copy.start()

    open_next(next_first)
    open_side(no(right_first), 0, True)
    open_side(no(left_first), 1, True)
    open_z(no(jnp.logical_or(held, last)))

    open_next(no(next_first))
    pltpu.make_async_copy(txt.at[pl.ds(0, 2 * ROWS)], txt.at[pl.ds(0, 2 * ROWS)], local_sem.at[3]).wait()
    columns(0)
    arrived(0)
    start_if(direct_to, direct)

    @pl.when(outlet)
    def _():
        z_img[0].wait_recv()
        next_other[0].start()

    arrived(1)
    open_z(held)

    @pl.when(outlet)
    def _():
        for got, copy in zip(z_img[1:], next_other[1:]):
            got.wait_recv()
            copy.start()

    arrived(2)
    pass_on(both(inlet, no(zero)), 3)
    arrived(3)

    def z_arrived(condition):
        @pl.when(condition)
        def _():
            for copy in z_img:
                copy.wait_recv()

            @pl.when(no(last))
            def _():
                for copy in next_other:
                    copy.start()

    z_arrived(no(jnp.logical_or(outlet, beside)))
    turn(0)
    columns(1, 2)
    arrived(4)
    pass_on(both(inlet, no(zero)), 2)
    arrived(5)
    z_arrived(beside)
    turn(1)
    arrived(6)
    pass_on(both(origin, behind), 3)
    arrived(7)
    pass_on(both(origin, no(behind)), 3)
    columns(3, 4)
    arrived(8, 9)
    near = sorted([(5, part) for part in FAR[0]] + [(6, part) for part in FAR[1]])
    far = sorted([(5, part) for part in FAR[1]] + [(6, part) for part in FAR[0]])

    @pl.when(no(inlet))
    def _():
        image_arrived(2)
        image_arrived(3)

    @pl.when(origin)
    def _():
        image_arrived(2)

    turn(2)
    turn(3)
    arrived(10)
    columns(5, 6)
    scores(near)
    contribution(near)
    reduce_step(0, 1)
    scores(whole(0, 1, 2, 3, 4))
    arrived(11)
    scores(far)
    arrived(12)
    columns(7)
    opposite = sorted((7, part) for d in range(2) for part in FAR[d][:STEP])
    scores(opposite)
    contribution(opposite)
    reduce_step(2)
    contribution(whole(3, 4))
    contribution(far)
    arrived(13)
    opposite = sorted((7, part) for d in range(2) for part in FAR[d][STEP:])
    scores(opposite)
    contribution(opposite)
    held_back = both(lax.rem(b, 2) == 1, b != n_blk - RUN - 1)

    @pl.when(held_back)
    def _():
        g1[...] = image_term(1)

    reduce_step(3, 4)

    @pl.when(no(held_back))
    def _():
        g1[...] = image_term(1)


    @pl.when(jnp.logical_not(inlet))
    def _():
        for j in (2, 3, 0, 1):
            gis[half(j), :] = g1[half(j), :].astype(BF16)
            back[j].start()

    @pl.when(jnp.logical_not(has_next))
    def _():
        gir[0 : 2 * ROWS, :] = jnp.zeros((2 * ROWS, gir.shape[1]), BF16)

    contribution(whole(1, 2))
    g0[...] = image_term(0)
    contribution(whole(0))
    reduce_step(5, 6, 7)
    inlet_back(no(zero), 0)
    inlet_back(no(zero), 1)
    reduce_step(8)
    own_back(no(outlet), 0, 1)
    reduce_step(9)
    inlet_back(no(zero), 2)
    reduce_step(10)
    inlet_back(no(zero), 3)
    reduce_step(11)
    inlet_back(zero, 0)
    inlet_back(zero, 1)
    reduce_step(12, 13)
    inlet_back(zero, 2)
    inlet_back(zero, 3)
    own_back(outlet, 0, 1)

    @pl.when(has_next)
    def _():
        back_wait(0)
        back_wait(1)

    for copy in z_own:
        copy.wait_recv()
    gi_out[0] = (scale * (g0[:ROWS, :] + gir[:ROWS, :].astype(F32) + zr[...].astype(F32))).astype(BF16)
    for part in sorted(range(PARTS), key=lambda part: r_orders[0].index((1, part)) + r_orders[1].index((1, part))):
        total = ct[part * CHUNK : (part + 1) * CHUNK, :]
        for d in range(2):
            m = r_orders[d].index((1, part))
            reduction[d][m].wait_recv()
            total = total + rrecv[d, m * CHUNK : (m + 1) * CHUNK, :].astype(F32)
        gt_out[0, part * CHUNK : (part + 1) * CHUNK, :] = (scale * total).astype(BF16)

    def all_sent(ref, sem):
        pltpu.make_async_copy(ref, ref, sem).wait()

    def images_sent(condition, count):
        @pl.when(condition)
        def _():
            all_sent(txt.at[pl.ds(0, count * ROWS)], im_s)
            all_sent(col.at[pl.ds(0, count)], me_s)

    all_sent(rrecv, ag_s)
    all_sent(rrecv, rs_s)
    all_sent(col.at[pl.ds(0, 7)], co_s)
    all_sent(gis, gi_s)
    all_sent(zs, zz_s)
    images_sent(no(jnp.logical_or(has_next, direct_to)), 1)
    images_sent(direct_to, 2)
    images_sent(both(has_next, no(inlet)), 3)
    images_sent(both(inlet, zero), 4)
    images_sent(both(inlet, no(zero)), 5)


def write(gi, gt, gi_out, gt_out, sems):
    copies = [
        pltpu.make_async_copy(src, dst, sems.at[i])
        for i, (src, dst) in enumerate(((gi, gi_out), (gt, gt_out)))
    ]
    for copy in copies:
        copy.start()
    for copy in copies:
        copy.wait()


def body(image, text, logit_scale, lse_row, lse_col, pair):
    width = image.shape[2]
    msgs = 3 * PARTS + PARTS // 2
    hbm = pl.BlockSpec(memory_space=pltpu.HBM)
    dma = pltpu.SemaphoreType.DMA
    vmem = pl.BlockSpec(memory_space=pltpu.VMEM)
    out = pltpu.VMEM((1, ROWS, width), BF16)
    grads = pl.pallas_call(
        kernel,
        out_shape=(out, out),
        in_specs=[hbm, hbm, pl.BlockSpec(memory_space=pltpu.SMEM), hbm, hbm, hbm],
        out_specs=(vmem, vmem),
        scratch_shapes=[
            pltpu.VMEM((PLACES * ROWS, width), BF16),
            pltpu.VMEM((4 * ROWS, width), BF16),
            pltpu.VMEM((width, 4 * ROWS), BF16),
            pltpu.VMEM((4, 8, ROWS), F32),
            pltpu.VMEM((PLACES, 8, ROWS), F32),
            pltpu.VMEM((PLACES * ROWS, ROWS), F32),
            pltpu.VMEM((PLACES * ROWS, 4 * ROWS), BF16),
            pltpu.VMEM((PLACES * ROWS, width), F32),
            pltpu.VMEM((2, msgs * CHUNK, width), BF16),
            pltpu.VMEM((2, msgs * CHUNK, width), BF16),
            pltpu.VMEM((2 * ROWS, width), F32),
            pltpu.VMEM((2 * ROWS, width), F32),
            pltpu.VMEM((2 * ROWS, width), BF16),
            pltpu.VMEM((4 * ROWS, width), BF16),
            pltpu.VMEM((ROWS, width), BF16),
            pltpu.VMEM((ROWS, width), BF16),
            pltpu.VMEM((2, 1, ROWS), BF16),
            pltpu.VMEM((1, ROWS), jnp.int32),
            pltpu.SemaphoreType.REGULAR((4,)),
            dma((4,)),
            dma,
            dma,
            dma((2, msgs)),
            dma,
            dma((6,)),
            dma,
            dma((3,)),
            dma,
            dma((2, 4)),
            dma,
            dma((8,)),
            dma,
            dma((2,)),
        ],
        compiler_params=pltpu.CompilerParams(
            collective_id=0, has_side_effects=True, vmem_limit_bytes=63 * 2**20
        ),
        cost_estimate=pl.CostEstimate(
            flops=12 * ROWS * 16 * ROWS * width, bytes_accessed=8 * ROWS * width, transcendentals=8 * ROWS * 16 * ROWS
        ),
    )(image, text, jnp.reshape(logit_scale, (1,)), lse_row, lse_col, pair)
    return pl.pallas_call(
        write,
        out_shape=[jax.ShapeDtypeStruct((1, ROWS, width), BF16)] * 2,
        in_specs=[vmem, vmem],
        out_specs=[hbm, hbm],
        scratch_shapes=[dma((2,))],
        compiler_params=pltpu.CompilerParams(vmem_limit_bytes=2**20),
    )(*grads)


def solution(mesh):
    return jax.shard_map(
        body,
        mesh=mesh,
        in_specs=(
            P("blk", "grp", None),
            P("blk", "grp", None),
            P(),
            P("blk", "grp"),
            P("blk", "grp"),
            P("blk", "grp"),
        ),
        out_specs=(P("blk", "grp", None), P("blk", "grp", None)),
        check_vma=False,
    )
```

```python
import functools

import jax
import jax.numpy as jnp
from jax import lax
from jax.experimental import pallas as pl
from jax.experimental.pallas import tpu as pltpu
from jax.sharding import PartitionSpec as P

MESH = pl.DeviceIdType.MESH
RING = 8
ROWS = 128
PARTS = 4
STEP = PARTS // 4
CHUNK = ROWS // PARTS
HALF = ROWS // 2
PLACES = 8
RUN = 8
FAR = ((2, 3), (1, 0))
F32 = jnp.float32
BF16 = jnp.bfloat16


def place(direction, hops):
    return 0 if hops == 0 else 7 if hops == 4 else 2 * hops - 1 + direction


def gather_order(direction):
    far, near = FAR[direction], FAR[1 - direction]
    order = [(hop, part) for hop in (1, 2, 3) for part in far + near]
    return order + [(4, part) for part in far]


def reduce_order(direction):
    f0, f1 = FAR[direction][:STEP], FAR[direction][STEP:]
    n0, n1 = FAR[1 - direction][:STEP], FAR[1 - direction][STEP:]
    order = [
        (3, n0), (3, n1), (4, f0), (4, f1), (2, n0), (3, f0), (3, f1),
        (2, n1), (2, f0), (2, f1), (1, n0), (1, n1), (1, f0), (1, f1),
    ]
    return [(hops, part) for hops, parts in order for part in parts]


def kernel(
    image, text, scale_ref, lrow_ref, lcol_ref, pair_ref, gi_out, gt_out,
    txt, img, imgt, meta, col, lct, dt, ct, rsend, rrecv, g0, g1, gis, gir, zs, zr, vecs, pairs,
    ready, local_sem, ag_s, rs_s, ring_r, im_s, im_r, me_s, me_r, co_s, co_r, gi_s, gi_r, zz_s, zz_r,
):
    g = lax.axis_index("grp")
    b = lax.axis_index("blk")
    n_blk = lax.axis_size("blk")
    n_grp = 2 * RING
    zpart = g + 1 - 2 * lax.rem(g, 2)
    nxt = lax.rem(b + 1, n_blk)
    prv = lax.rem(b + n_blk - 1, n_blk)
    ring = [lax.rem(g + 2 * i, n_grp) for i in range(RING)]
    side = [ring[1], ring[7]]
    z_lo = lax.rem(g, 2)
    last = lax.rem(b, RUN) == RUN - 1
    first = lax.rem(b, RUN) == 0
    zero = b == 0
    low, high = z_lo == 0, z_lo == 1
    no = jnp.logical_not
    both = jnp.logical_and
    has_next = no(both(last, low))
    has_prev = no(both(first, high))
    outlet = both(last, high)
    inlet = both(first, low)
    next_grp = jnp.where(last, zpart, g)
    prev_grp = jnp.where(first, zpart, g)

    y = g // 2
    origin = both(zero, low)
    left_first = jnp.where(y == 0, origin, both(y < 7, no(both(origin, y == 1))))
    right_first = jnp.where(y == 0, origin, jnp.where(y == 7, no(origin), y == 6))
    z_first = jnp.where(jnp.logical_or(both(zero, y == 0), nxt == 0), low, high)
    early = lambda blk: jnp.logical_or(blk == 0, blk == n_blk - RUN)
    prev_first = both(has_prev, no(jnp.logical_or(early(b), both(b == 1, both(y == 0, low)))))
    next_first = both(has_next, jnp.logical_or(early(nxt), both(origin, y == 0)))
    direct_from = both(zero, high)
    direct_to = both(nxt == 0, low)
    meets = (
        (left_first, True, side[1], b, 1),
        (right_first, True, side[0], b, 0),
        (z_first, True, zpart, b, 2),
        (prev_first, has_prev, prev_grp, prv, 3),
        (next_first, has_next, next_grp, nxt, None),
        (direct_to, direct_from, zpart, prv, None),
    )
    barrier = pltpu.get_barrier_semaphore()

    def greet(grp, blk, sem):
        pl.semaphore_signal(sem, inc=1, device_id={"grp": grp, "blk": blk}, device_id_type=MESH)

    for they_first, met, grp, blk, _ in meets:

        @pl.when(both(met, no(they_first)))
        def _(grp=grp, blk=blk):
            greet(grp, blk, barrier)

    def copy_to(src, dst, s_sem, r_sem, grp=g, blk=b):
        return pltpu.make_async_remote_copy(
            src_ref=src, dst_ref=dst, send_sem=s_sem, recv_sem=r_sem,
            device_id={"grp": grp, "blk": blk}, device_id_type=MESH,
        )

    local = [
        pltpu.make_async_copy(src, dst, local_sem.at[min(i, 3)])
        for i, (src, dst) in enumerate((
            (pair_ref, pairs),
            (lrow_ref, vecs.at[0]),
            (lcol_ref, vecs.at[1]),
            (text.at[0], txt.at[pl.ds(0, ROWS)]),
            (image.at[0], img.at[pl.ds(0, ROWS)]),
        ))
    ]
    for copy in local:
        copy.start()
    scale = scale_ref[0]

    def go(copy):
        copy.start()

    orders = [gather_order(0), gather_order(1)]

    def gather_copy(direction, n):
        hop, part = orders[direction][n]
        rows = lambda p: txt.at[pl.ds(p * ROWS + part * CHUNK, CHUNK)]
        src = text.at[0, pl.ds(part * CHUNK, CHUNK)] if hop == 1 else rows(place(direction, hop - 1))
        return copy_to(
            src, rows(place(direction, hop)), ag_s, ring_r.at[direction, n], grp=side[direction]
        )

    def col_copy(direction, hop):
        return copy_to(
            col.at[place(direction, hop - 1)], col.at[place(direction, hop)],
            co_s, co_r.at[direction, hop - 1], grp=side[direction],
        )

    gather = [[gather_copy(d, n) for n in range(len(orders[d]))] for d in range(2)]
    cols = [[col_copy(0, hop) for hop in (1, 2, 3, 4)], [col_copy(1, hop) for hop in (1, 2, 3)]]

    def arrived(*steps):
        for n in [STEP * step + i for step in steps for i in range(STEP)]:
            hop = n // PARTS + 1
            for d in range(2):
                if n % PARTS == 0 and hop <= len(cols[d]):
                    cols[d][hop - 1].wait_recv()
                    if hop < len(cols[d]):
                        go(cols[d][hop])
                gather[d][n].wait_recv()
                if n + PARTS < len(orders[d]):
                    go(gather[d][n + PARTS])

    def image_copies(src, dst, **to):
        def copy(i):
            start = i * HALF
            rows = image.at[0, pl.ds(start, HALF)] if src == 0 else img.at[pl.ds(src * ROWS + start, HALF)]
            r_sem = im_r.at[2 * (dst - 1) + i]
            return copy_to(rows, img.at[pl.ds(dst * ROWS + start, HALF)], im_s, r_sem, **to)

        return copy(0), copy(1), copy_to(meta.at[src], meta.at[dst], me_s, me_r.at[dst - 1], **to)

    swap = last.astype(jnp.int32)
    z_img = image_copies(0, 1, grp=zpart)
    next_own = image_copies(0, 2 + swap, grp=next_grp, blk=nxt)
    next_other = image_copies(1, 3 - swap, grp=next_grp, blk=nxt)
    passed = {3: image_copies(3, 2, grp=zpart), 2: image_copies(2, 3, grp=zpart)}
    direct = image_copies(0, 3, grp=zpart, blk=nxt)
    arrivals = {2: image_copies(0, 2, grp=zpart), 3: image_copies(0, 3, grp=zpart)}

    def image_arrived(slot):
        for copy in arrivals[slot]:
            copy.wait_recv()

    def start_if(condition, copies):
        @pl.when(condition)
        def _():
            for copy in copies:
                copy.start()

    def pass_on(condition, slot):
        @pl.when(condition)
        def _():
            for got, copy in zip(arrivals[slot], passed[slot]):
                got.wait_recv()
                copy.start()

    def take(ref, parts):
        pieces = []
        for p, part in parts:
            lo = p * ROWS + part * CHUNK
            if pieces and pieces[-1][1] == lo:
                pieces[-1][1] = lo + CHUNK
            else:
                pieces.append([lo, lo + CHUNK])
        pieces = [ref[lo:hi, :] for lo, hi in pieces]
        return pieces[0] if len(pieces) == 1 else jnp.concatenate(pieces, axis=0)

    def whole(*places):
        return [(p, part) for p in places for part in range(PARTS)]

    def columns(*places):
        for p in places:
            lct[p * ROWS : (p + 1) * ROWS, :] = jnp.broadcast_to(col[p, 0:1, :], (ROWS, ROWS)).T

    def turn(slot):
        imgt[:, slot * ROWS : (slot + 1) * ROWS] = img[slot * ROWS : (slot + 1) * ROWS, :].T

    def scores(parts):
        s = jnp.dot(take(txt, parts), imgt[...], preferred_element_type=F32) * scale
        lr = jnp.concatenate([meta[slot, 0:1, :] for slot in range(4)], axis=1)
        lc = take(lct, parts)
        d = 0.5 * (jnp.exp(s - lr) + jnp.exp(s - jnp.concatenate([lc] * 4, axis=1)))
        pr = jnp.concatenate([meta[0, 1:2, :], meta[1, 1:2, :]], axis=1).astype(jnp.int32)
        iota = lax.broadcasted_iota(jnp.int32, (CHUNK, 2 * ROWS), 0)
        for i, (p, part) in enumerate(parts):
            rel = 0 if p == 0 else 4 if p == 7 else (RING - (p + 1) // 2) if p % 2 else p // 2
            rows = d[i * CHUNK : (i + 1) * CHUNK]
            own = rows[:, : 2 * ROWS] - (pr - (ring[rel] * ROWS + part * CHUNK) == iota).astype(F32)
            lo = p * ROWS + part * CHUNK
            dt[lo : lo + CHUNK, : 2 * ROWS] = own.astype(BF16)
            dt[lo : lo + CHUNK, 2 * ROWS :] = rows[:, 2 * ROWS :].astype(BF16)

    def contribution(parts):
        c = jnp.dot(take(dt, parts), img[...], preferred_element_type=F32)
        for i, (p, part) in enumerate(parts):
            lo = p * ROWS + part * CHUNK
            ct[lo : lo + CHUNK, :] = c[i * CHUNK : (i + 1) * CHUNK]

    def image_term(k):
        return lax.dot_general(
            dt[:, k * 2 * ROWS : (k + 1) * 2 * ROWS], txt[...], (((0,), (0,)), ((), ())), preferred_element_type=F32
        )

    r_orders = [reduce_order(0), reduce_order(1)]

    def reduce_copy(direction, n):
        rows = pl.ds(n * CHUNK, CHUNK)
        return copy_to(
            rsend.at[direction, rows], rrecv.at[direction, rows],
            rs_s, ring_r.at[direction, n], grp=side[direction],
        )

    reduction = [[reduce_copy(d, n) for n in range(len(r_orders[d]))] for d in range(2)]

    def reduce_step(*steps):
        for n in [STEP * step + i for step in steps for i in range(STEP)]:
            for d in range(2):
                hops, part = r_orders[d][n]
                start = place(1 - d, hops) * ROWS + part * CHUNK
                total = ct[start : start + CHUNK, :]
                if (hops + 1, part) in r_orders[d]:
                    m = r_orders[d].index((hops + 1, part))
                    reduction[d][m].wait_recv()
                    total = total + rrecv[d, m * CHUNK : (m + 1) * CHUNK, :].astype(F32)
                rsend[d, n * CHUNK : (n + 1) * CHUNK, :] = total.astype(BF16)
                go(reduction[d][n])

    half = lambda j: slice(j * HALF, (j + 1) * HALF)
    feeder = jnp.logical_and(first, z_lo == 1)
    back_blk = jnp.where(feeder, b, prv)

    def back_copy(j):
        if j < 2:
            to = jnp.where(feeder, j + 6, jnp.where(inlet, j + 2, j))
        else:
            to = jnp.where(feeder, j + 2, jnp.where(inlet, j - 2, j))
        return copy_to(
            gis.at[pl.ds(j * HALF, HALF)], gir.at[pl.ds(pl.multiple_of(to * HALF, HALF), HALF)],
            gi_s, gi_r.at[to], grp=prev_grp, blk=back_blk,
        )

    back = [back_copy(j) for j in range(4)]

    def back_wait(to):
        rows = pl.ds(to * HALF, HALF)
        copy_to(gis.at[pl.ds(0, HALF)], gir.at[rows], gi_s, gi_r.at[to], grp=zpart).wait_recv()

    def inlet_back(condition, j):
        @pl.when(both(inlet, condition))
        def _():
            back_wait(4 + j)
            gis[half(j), :] = (g1[half(j), :] + gir[half(4 + j), :].astype(F32)).astype(BF16)
            back[j].start()

    z_own = [
        copy_to(zs.at[pl.ds(i * HALF, HALF)], zr.at[pl.ds(i * HALF, HALF)], zz_s, zz_r.at[i], grp=zpart)
        for i in range(2)
    ]

    def own_back(condition, *halves):
        @pl.when(condition)
        def _():
            for i in halves:

                @pl.when(has_next)
                def _():
                    back_wait(2 + i)

                zs[half(i), :] = (g0[half(2 + i), :] + gir[half(2 + i), :].astype(F32)).astype(BF16)
                z_own[i].start()

    behind = jnp.logical_or(y < 2, y == RING - 1)

    greeted = sum(they_first.astype(jnp.int32) for they_first, *_ in meets)

    @pl.when(greeted > 0)
    def _():
        pl.semaphore_wait(barrier, greeted)

    for they_first, _, grp, blk, sem in meets:
        if sem is not None:

            @pl.when(they_first)
            def _(grp=grp, blk=blk, sem=sem):
                greet(grp, blk, ready.at[sem])

    for copy in local[:3]:
        copy.wait()
    meta[0] = jnp.zeros((8, ROWS), F32)
    meta[0, 0:1, :] = vecs[0].astype(F32)
    meta[0, 1:2, :] = pairs[...].astype(F32)
    col[0] = jnp.broadcast_to(vecs[1].astype(F32), (8, ROWS))

    def open_side(condition, d, answer):
        @pl.when(condition)
        def _():
            if answer:
                pl.semaphore_wait(ready.at[1 - d], 1)
            cols[d][0].start()
            for n in range(PARTS):
                gather[d][n].start()

    open_side(left_first, 1, False)
    open_side(right_first, 0, False)
    beside = lax.rem(b, RUN) == RUN - 2
    held = jnp.logical_or(beside, both(both(zero, y == 0), high))

    def open_z(condition):
        @pl.when(condition)
        def _():
            @pl.when(no(z_first))
            def _():
                pl.semaphore_wait(ready.at[2], 1)

            for copy in z_img:
                copy.start()

    open_z(last)

    def open_next(condition):
        @pl.when(both(has_next, condition))
        def _():
            @pl.when(no(next_first))
            def _():
                pl.semaphore_wait(ready.at[3], 1)

            for copy in next_own:
                copy.start()

    open_next(next_first)
    open_side(no(right_first), 0, True)
    open_side(no(left_first), 1, True)
    open_z(no(jnp.logical_or(held, last)))

    open_next(no(next_first))
    pltpu.make_async_copy(txt.at[pl.ds(0, 2 * ROWS)], txt.at[pl.ds(0, 2 * ROWS)], local_sem.at[3]).wait()
    columns(0)
    arrived(0)
    start_if(direct_to, direct)

    @pl.when(outlet)
    def _():
        z_img[0].wait_recv()
        next_other[0].start()

    arrived(1)
    open_z(held)

    @pl.when(outlet)
    def _():
        for got, copy in zip(z_img[1:], next_other[1:]):
            got.wait_recv()
            copy.start()

    arrived(2)
    pass_on(both(inlet, no(zero)), 3)
    arrived(3)

    def z_arrived(condition):
        @pl.when(condition)
        def _():
            for copy in z_img:
                copy.wait_recv()

            @pl.when(no(last))
            def _():
                for copy in next_other:
                    copy.start()

    z_arrived(no(jnp.logical_or(outlet, beside)))
    turn(0)
    columns(1, 2)
    arrived(4)
    pass_on(both(inlet, no(zero)), 2)
    arrived(5)
    z_arrived(beside)
    turn(1)
    arrived(6)
    pass_on(both(origin, behind), 3)
    arrived(7)
    pass_on(both(origin, no(behind)), 3)
    columns(3, 4)
    arrived(8, 9)
    near = sorted([(5, part) for part in FAR[0]] + [(6, part) for part in FAR[1]])
    far = sorted([(5, part) for part in FAR[1]] + [(6, part) for part in FAR[0]])

    columns(5, 6)

    @pl.when(no(inlet))
    def _():
        image_arrived(2)
        image_arrived(3)

    @pl.when(origin)
    def _():
        image_arrived(2)

    turn(2)
    turn(3)
    arrived(10)
    scores(near)
    contribution(near)
    reduce_step(0, 1)

    @pl.when(no(zero))
    def _():
        scores(whole(0, 1, 2, 3, 4))

    arrived(11)

    @pl.when(no(zero))
    def _():
        scores(far)

    arrived(12)
    columns(7)
    opposite = sorted((7, part) for d in range(2) for part in FAR[d][:STEP])
    scores(opposite)
    contribution(opposite)
    reduce_step(2)

    @pl.when(no(zero))
    def _():
        contribution(whole(3, 4))
        contribution(far)

    arrived(13)
    opposite = sorted((7, part) for d in range(2) for part in FAR[d][STEP:])
    scores(opposite)
    contribution(opposite)
    held_back = both(lax.rem(b, 2) == 1, b != n_blk - RUN - 1)

    @pl.when(held_back)
    def _():
        g1[...] = image_term(1)

    reduce_step(3)

    @pl.when(zero)
    def _():
        scores(whole(0, 1, 2, 3, 4))
        scores(far)
        contribution(whole(3, 4))
        contribution(far)

    reduce_step(4)

    @pl.when(no(held_back))
    def _():
        g1[...] = image_term(1)


    @pl.when(jnp.logical_not(inlet))
    def _():
        for j in (2, 3, 0, 1):
            gis[half(j), :] = g1[half(j), :].astype(BF16)
            back[j].start()

    @pl.when(jnp.logical_not(has_next))
    def _():
        gir[0 : 2 * ROWS, :] = jnp.zeros((2 * ROWS, gir.shape[1]), BF16)

    contribution(whole(1, 2))
    g0[...] = image_term(0)
    contribution(whole(0))
    reduce_step(5, 6, 7)
    inlet_back(no(zero), 0)
    inlet_back(no(zero), 1)
    reduce_step(8)
    own_back(no(outlet), 0, 1)
    reduce_step(9)
    inlet_back(no(zero), 2)
    reduce_step(10)
    inlet_back(no(zero), 3)
    reduce_step(11)
    inlet_back(zero, 0)
    inlet_back(zero, 1)
    reduce_step(12, 13)
    inlet_back(zero, 2)
    inlet_back(zero, 3)
    own_back(outlet, 0, 1)

    @pl.when(has_next)
    def _():
        back_wait(0)
        back_wait(1)

    for copy in z_own:
        copy.wait_recv()
    gi_out[0] = (scale * (g0[:ROWS, :] + gir[:ROWS, :].astype(F32) + zr[...].astype(F32))).astype(BF16)
    for part in sorted(range(PARTS), key=lambda part: r_orders[0].index((1, part)) + r_orders[1].index((1, part))):
        total = ct[part * CHUNK : (part + 1) * CHUNK, :]
        for d in range(2):
            m = r_orders[d].index((1, part))
            reduction[d][m].wait_recv()
            total = total + rrecv[d, m * CHUNK : (m + 1) * CHUNK, :].astype(F32)
        gt_out[0, part * CHUNK : (part + 1) * CHUNK, :] = (scale * total).astype(BF16)

    def all_sent(ref, sem):
        pltpu.make_async_copy(ref, ref, sem).wait()

    def images_sent(condition, count):
        @pl.when(condition)
        def _():
            all_sent(txt.at[pl.ds(0, count * ROWS)], im_s)
            all_sent(col.at[pl.ds(0, count)], me_s)

    all_sent(rrecv, ag_s)
    all_sent(rrecv, rs_s)
    all_sent(col.at[pl.ds(0, 7)], co_s)
    all_sent(gis, gi_s)
    all_sent(zs, zz_s)
    images_sent(no(jnp.logical_or(has_next, direct_to)), 1)
    images_sent(direct_to, 2)
    images_sent(both(has_next, no(inlet)), 3)
    images_sent(both(inlet, zero), 4)
    images_sent(both(inlet, no(zero)), 5)


def write(gi, gt, gi_out, gt_out, sems):
    copies = [
        pltpu.make_async_copy(src, dst, sems.at[i])
        for i, (src, dst) in enumerate(((gi, gi_out), (gt, gt_out)))
    ]
    for copy in copies:
        copy.start()
    for copy in copies:
        copy.wait()


def body(image, text, logit_scale, lse_row, lse_col, pair):
    width = image.shape[2]
    msgs = 3 * PARTS + PARTS // 2
    hbm = pl.BlockSpec(memory_space=pltpu.HBM)
    dma = pltpu.SemaphoreType.DMA
    vmem = pl.BlockSpec(memory_space=pltpu.VMEM)
    out = pltpu.VMEM((1, ROWS, width), BF16)
    grads = pl.pallas_call(
        kernel,
        out_shape=(out, out),
        in_specs=[hbm, hbm, pl.BlockSpec(memory_space=pltpu.SMEM), hbm, hbm, hbm],
        out_specs=(vmem, vmem),
        scratch_shapes=[
            pltpu.VMEM((PLACES * ROWS, width), BF16),
            pltpu.VMEM((4 * ROWS, width), BF16),
            pltpu.VMEM((width, 4 * ROWS), BF16),
            pltpu.VMEM((4, 8, ROWS), F32),
            pltpu.VMEM((PLACES, 8, ROWS), F32),
            pltpu.VMEM((PLACES * ROWS, ROWS), F32),
            pltpu.VMEM((PLACES * ROWS, 4 * ROWS), BF16),
            pltpu.VMEM((PLACES * ROWS, width), F32),
            pltpu.VMEM((2, msgs * CHUNK, width), BF16),
            pltpu.VMEM((2, msgs * CHUNK, width), BF16),
            pltpu.VMEM((2 * ROWS, width), F32),
            pltpu.VMEM((2 * ROWS, width), F32),
            pltpu.VMEM((2 * ROWS, width), BF16),
            pltpu.VMEM((4 * ROWS, width), BF16),
            pltpu.VMEM((ROWS, width), BF16),
            pltpu.VMEM((ROWS, width), BF16),
            pltpu.VMEM((2, 1, ROWS), BF16),
            pltpu.VMEM((1, ROWS), jnp.int32),
            pltpu.SemaphoreType.REGULAR((4,)),
            dma((4,)),
            dma,
            dma,
            dma((2, msgs)),
            dma,
            dma((6,)),
            dma,
            dma((3,)),
            dma,
            dma((2, 4)),
            dma,
            dma((8,)),
            dma,
            dma((2,)),
        ],
        compiler_params=pltpu.CompilerParams(
            collective_id=0, has_side_effects=True, vmem_limit_bytes=63 * 2**20
        ),
        cost_estimate=pl.CostEstimate(
            flops=12 * ROWS * 16 * ROWS * width, bytes_accessed=8 * ROWS * width, transcendentals=8 * ROWS * 16 * ROWS
        ),
    )(image, text, jnp.reshape(logit_scale, (1,)), lse_row, lse_col, pair)
    return pl.pallas_call(
        write,
        out_shape=[jax.ShapeDtypeStruct((1, ROWS, width), BF16)] * 2,
        in_specs=[vmem, vmem],
        out_specs=[hbm, hbm],
        scratch_shapes=[dma((2,))],
        compiler_params=pltpu.CompilerParams(vmem_limit_bytes=2**20),
    )(*grads)


def solution(mesh):
    return jax.shard_map(
        body,
        mesh=mesh,
        in_specs=(
            P("blk", "grp", None),
            P("blk", "grp", None),
            P(),
            P("blk", "grp"),
            P("blk", "grp"),
            P("blk", "grp"),
        ),
        out_specs=(P("blk", "grp", None), P("blk", "grp", None)),
        check_vma=False,
    )
```
